512 devices in a mesh: text: 16 (over y, x_hi, core), vis: 32 (over z, x_lo).
Axes of the slice: x: 4 (x_hi: 2, x_lo: 2; x = x_hi * 2 + x_lo), y: 4, z: 16, core: 2. Of those that a mesh axis runs over, the one named last changes fastest.
Arguments:
- text_rows: bfloat16 [512, 4096], P('text', 'vis'), may hold values from -6 to 6
- visual: bfloat16 [16384, 4096], P('vis', 'text'), may hold values from -9 to 9
- norm_gain: float32 [4096], replicated, may hold values from 0.25 to 1.75
- q_weight: bfloat16 [4096, 4096], P(None, 'vis'), may hold values from -0.09375 to 0.09375
- key_value_weight: bfloat16 [4096, 2048], P(None, 'text'), may hold values from -0.09375 to 0.09375
- q_gain: float32 [128], replicated, may hold values from 0.8 to 8
- k_gain: float32 [128], replicated, may hold values from 0.8 to 8
- out_weight: bfloat16 [4096, 4096], P('vis'), may hold values from -0.29882812 to 0.29882812
- attn_gate: float32 [1], replicated, may hold values from 0.6 to 1.5
Outputs:
- gated: bfloat16 [512, 4096], P('text', 'vis')
The draws below stay inside these ranges and needn't reach their ends.
All inputs are finite; a program needn't handle non-finite values.
Results may differ from the reference program's by a relative error of at most 0.007.
The reference program's roundings to bfloat16 on the way count: a program that leaves them out, or rounds other values in their place, can miss the bound.
Values may be sent and summed in bfloat16 or wider, within the bound.
A program may use at most 64 MiB of HBM per device.

```python
import jax
import jax.numpy as jnp
from jax import lax

MODEL_WIDTH = 4096
QUERY_HEAD_COUNT = 32
KEY_VALUE_HEADS = 8
HEAD_SIZE = 128
VISUAL_PER_INDEX = 512
TEXT_ROW_TOTAL = 512
VISUAL_TOKENS = 16384
N_VIS = 32


def strong_mask(key):
    order = jax.random.permutation(key, HEAD_SIZE)
    return order < max(1, HEAD_SIZE // 8)


def gain_law(key, low, high, mask):
    base = jnp.exp(jax.random.uniform(key, (HEAD_SIZE,), jnp.float32, jnp.log(low), jnp.log(high)))
    return jnp.where(mask, jnp.float32(8.0), base)


def draw_q_gain(key, part):
    mask = strong_mask(jax.random.fold_in(key, 5))
    key = jax.random.fold_in(key, 11)
    return gain_law(key, 0.8, 2.5, mask)


def draw_k_gain(key, part):
    mask = strong_mask(jax.random.fold_in(key, 5))
    key = jax.random.fold_in(key, 23)
    return gain_law(key, 0.8, 2.5, mask)


def draw_visual(key, part):
    key = jax.random.fold_in(key, 37)
    noise_key = jax.random.fold_in(key, 0)
    noise = jax.random.normal(noise_key, (VISUAL_TOKENS, MODEL_WIDTH), jnp.float32)
    return jnp.clip(noise, -6.0, 6.0).astype(jnp.bfloat16)


def block_scale(own_key, dims, cuts, low, largest):
    level, own = 1.0, jax.random.fold_in(own_key, 6)
    for dim, blocks in cuts:
        draws = jnp.exp(jax.random.uniform(jax.random.fold_in(own, dim), (blocks,), jnp.float32, low / len(cuts), largest / len(cuts)))
        level = level * jnp.repeat(draws, dims[dim] // blocks).reshape([-1 if axis == dim else 1 for axis in range(len(dims))])
    return level


def centred(stream_key, shape, width, reach, shards=(), dtype=jnp.bfloat16):
    drawn = jax.random.normal(stream_key, shape, jnp.float32) * width
    if len(shards) > 0:
        drawn = block_scale(stream_key, shape, shards, -0.22, 0.18) * drawn
    return jnp.clip(drawn, min=-reach, max=reach).astype(dtype)


def setup_inputs(seed: int = 0) -> dict:
    streams_of = jax.random.split(jax.random.key(seed), 10)
    text_rows = centred(streams_of[0], (TEXT_ROW_TOTAL, MODEL_WIDTH), 1.0, 6.0, ((0, 16), (1, 32)))
    visual = draw_visual(jax.random.fold_in(streams_of[9], 71), 0)
    norm_gain = jnp.clip(1.0 + 0.15 * jax.random.normal(streams_of[2], (MODEL_WIDTH,), jnp.float32), 0.25, 1.75)
    q_weight = centred(streams_of[3], (MODEL_WIDTH, QUERY_HEAD_COUNT * HEAD_SIZE), MODEL_WIDTH ** -0.5, 0.09375, ((1, 32),))
    key_value_weight = centred(streams_of[4], (MODEL_WIDTH, 2 * KEY_VALUE_HEADS * HEAD_SIZE), MODEL_WIDTH ** -0.5, 0.09375, ((1, 16),))
    q_gain = draw_q_gain(jax.random.fold_in(streams_of[9], 71), 0)
    k_gain = draw_k_gain(jax.random.fold_in(streams_of[9], 71), 0)
    out_weight = centred(streams_of[7], (QUERY_HEAD_COUNT * HEAD_SIZE, MODEL_WIDTH), 0.05, 0.29882812, ((0, 32),))
    attn_gate = jnp.clip(jax.random.uniform(streams_of[8], (1,), jnp.float32, 0.6, 1.5), 0.6, 1.5)
    return {"text_rows": text_rows, "visual": visual, "norm_gain": norm_gain, "q_weight": q_weight, "key_value_weight": key_value_weight, "q_gain": q_gain, "k_gain": k_gain, "out_weight": out_weight, "attn_gate": attn_gate}


def head_norm(heads, gain):
    mean_square = lax.optimization_barrier(jnp.mean(heads * heads, axis=-1, keepdims=True))
    return heads * lax.rsqrt(mean_square + 1e-05) * gain

def reference(text_rows, visual, norm_gain, q_weight, key_value_weight, q_gain, k_gain, out_weight, attn_gate):
    scaled = (text_rows.astype(jnp.float32) * norm_gain).astype(jnp.bfloat16)
    query_raw = jnp.dot(scaled, q_weight, preferred_element_type=jnp.float32)
    query_rows = head_norm(query_raw.reshape(TEXT_ROW_TOTAL, QUERY_HEAD_COUNT, HEAD_SIZE), q_gain).astype(jnp.bfloat16)
    key_value_rows = jnp.dot(visual, key_value_weight, preferred_element_type=jnp.float32).astype(jnp.bfloat16)
    unscaled_keys = key_value_rows[:, :KEY_VALUE_HEADS * HEAD_SIZE].astype(jnp.float32).reshape(VISUAL_TOKENS, KEY_VALUE_HEADS, HEAD_SIZE)
    head_keys = head_norm(unscaled_keys, k_gain).astype(jnp.bfloat16)
    head_values = key_value_rows[:, KEY_VALUE_HEADS * HEAD_SIZE:].reshape(VISUAL_TOKENS, KEY_VALUE_HEADS, HEAD_SIZE)
    query_group_width = QUERY_HEAD_COUNT // KEY_VALUE_HEADS
    grouped_queries = query_rows.reshape(TEXT_ROW_TOTAL, KEY_VALUE_HEADS, query_group_width, HEAD_SIZE).astype(jnp.float32)
    key_block_list = head_keys.reshape(N_VIS, VISUAL_PER_INDEX, KEY_VALUE_HEADS, HEAD_SIZE)
    value_block_list = head_values.reshape(N_VIS, VISUAL_PER_INDEX, KEY_VALUE_HEADS, HEAD_SIZE)
    scale = 1.0 / jnp.sqrt(jnp.float32(HEAD_SIZE))

    def visit(carry, block):
        running, best, denom = carry
        key_block, value_block = block
        scores = jnp.einsum('rhgd,khd->rhgk', grouped_queries, key_block.astype(jnp.float32)) * scale
        block_peak = lax.optimization_barrier(jnp.max(scores, axis=-1))
        weights = jnp.exp(scores - block_peak[..., None])
        block_total = lax.optimization_barrier(jnp.sum(weights, axis=-1))
        weights_low = weights.astype(jnp.bfloat16).astype(jnp.float32)
        partial_value = jnp.einsum('rhgk,khd->rhgd', weights_low, value_block.astype(jnp.float32))
        new_best = jnp.maximum(best, block_peak)
        old_factor = jnp.exp(best - new_best)
        new_factor = jnp.exp(block_peak - new_best)
        running = running * old_factor[..., None] + partial_value * new_factor[..., None]
        denom = denom * old_factor + block_total * new_factor
        return ((running, new_best, denom), None)
    begin_index = (jnp.zeros((TEXT_ROW_TOTAL, KEY_VALUE_HEADS, query_group_width, HEAD_SIZE), jnp.float32), jnp.full((TEXT_ROW_TOTAL, KEY_VALUE_HEADS, query_group_width), -jnp.inf, jnp.float32), jnp.zeros((TEXT_ROW_TOTAL, KEY_VALUE_HEADS, query_group_width), jnp.float32))
    (running, best, denom), unused = lax.scan(visit, begin_index, (key_block_list, value_block_list))
    attended = (running / denom[..., None]).astype(jnp.bfloat16).reshape(TEXT_ROW_TOTAL, QUERY_HEAD_COUNT * HEAD_SIZE)
    projected = jnp.dot(attended, out_weight, preferred_element_type=jnp.float32)
    return (jnp.tanh(attn_gate[0]) * projected).astype(jnp.bfloat16)
```

```python
import jax
import jax.numpy as jnp
from jax import lax
from jax.experimental import pallas as pl
from jax.experimental.pallas import tpu as pltpu
from jax.sharding import PartitionSpec as P

HEAD = 128
EPS = 1e-05
SCALE_LOG2 = (HEAD ** -0.5) * 1.4426950408889634
MESH = pl.DeviceIdType.MESH
BF16 = jnp.bfloat16
F32 = jnp.float32


def rcopy(src, dst, send, recv, t, v):
    return pltpu.make_async_remote_copy(
        src_ref=src, dst_ref=dst, send_sem=send, recv_sem=recv, device_id=(t, v), device_id_type=MESH
    )


def head_norm(heads, gain):
    mean_square = jnp.mean(heads * heads, axis=-1, keepdims=True)
    return heads * lax.rsqrt(mean_square + EPS) * gain


def column_tile(m, l):
    lane = lax.broadcasted_iota(jnp.int32, (8, 128), 1)
    tile = jnp.zeros((8, 128), F32)
    for k in range(32):
        tile = jnp.where(lane == k, m[8 * k : 8 * k + 8], tile)
        tile = jnp.where(lane == 32 + k, l[8 * k : 8 * k + 8], tile)
    return tile


def kernel(
    text_ref, vis_ref, gain_ref, wq_hbm, wkv_hbm, qg_ref, kg_ref, wo_hbm, gate_ref,
    out_ref,
    text_s, text_all, wq, wk, vb, q_loc, qbuf, kvst, kvb,
    o_send, t_send, o_own, t_own, o_recv, t_recv, o2, t2, d_all, t_all,
    att, att_all, wo2, r_send, r_recv,
    loc, vsend, vrecv, wsend, wrecv, tsend, trecv, txsend, txrecv, c1send, c1recv,
    qsend, qfsend, qrecv, wosend, worecv, kvsend, kvrecv, osend, orecv, ssend, srecv,
    dsend, drecv, t2send, t2recv, asend, arecv, rsend, rrecv,
):
    t = lax.axis_index("text")
    v = lax.axis_index("vis")
    z = v // 2
    xl = v % 2
    c = t % 2
    half = t // 8
    g = t % 8
    vx = 2 * z + 1 - xl
    sib = t + 1 - 2 * c
    xh = (t // 2) % 2
    base = (t // 4) * 4
    xp = base + (1 - xh) * 2 + c
    xps = base + (1 - xh) * 2 + 1 - c
    up = (t + 4) % 16
    dn = (t + 12) % 16
    far = (t + 8) % 16
    col = t - c
    far_sib = (sib + 8) % 16
    t1 = half * 8 + v // 4
    v1 = g * 4 + v % 4
    v2 = g * 4 + (v % 4) + 1 - 2 * (v % 2)
    owner = g == v // 4
    j_own = v % 4

    def at_z(zz):
        return 2 * zz + xl

    def ring(i):
        return lax.rem(z + 8 + jnp.where(i % 2 == 0, -(i // 2), (i + 1) // 2), 16)

    def each_z(body):
        def step(i, carry):
            body(ring(i))
            return carry

        lax.fori_loop(0, 15, step, 0)

    own_tokens = pltpu.make_async_copy(vis_ref.at[pl.ds(c * 256, 256), :], vb.at[t], loc.at[0])
    own_wq = pltpu.make_async_copy(wq_hbm, wq, loc.at[1])
    own_wk = pltpu.make_async_copy(wkv_hbm, wk.at[:, pl.ds(pl.multiple_of(c * 128, 128), 128)], loc.at[2])
    own_tokens.start()
    own_wk.start()
    own_wq.start()
    gain = gain_ref[:, pl.ds(pl.multiple_of(v * 128, 128), 128)]
    text_s[...] = (text_ref[...].astype(F32) * gain).astype(BF16)
    my_cols = pl.ds(pl.multiple_of(z * 128, 128), 128)
    text_all[xl, :, my_cols] = text_s[...]

    barrier = pltpu.get_barrier_semaphore()

    def greet(tt, vv):
        pl.semaphore_signal(barrier, inc=1, device_id=(tt, vv), device_id_type=MESH)

    each_z(lambda zz: greet(t, at_z(zz)))
    greet(t, vx)
    for other in (sib, xp, up, dn, far, far_sib):
        greet(other, v)
    greet(t1, v2)

    @pl.when(owner)
    def _():
        def step(i, carry):
            greet(half * 8 + lax.rem(g + i, 8), v)
            return carry

        lax.fori_loop(1, 8, step, 0)

    @pl.when(jnp.logical_not(owner))
    def _():
        greet(t1, v)
        greet(t1, v1)

    pl.semaphore_wait(barrier, 15 + 1 + 6 + 1 + jnp.where(owner, 7, 2))

    rows_here = pl.ds(c * 256, 256)
    rows_sib = pl.ds((1 - c) * 256, 256)
    to_sib = rcopy(vis_ref.at[rows_sib, :], vb.at[t], vsend.at[0], vrecv.at[t], sib, v)
    to_sib.start()

    def push_text(zz):
        rcopy(text_s, text_all.at[xl, :, my_cols], tsend, trecv, t, at_z(zz)).start()

    each_z(push_text)
    sends = [to_sib]

    def send_block(f, target, src=None):
        copy = rcopy(
            vb.at[f] if src is None else src, vb.at[f], vsend.at[len(sends)], vrecv.at[f], target, v
        )
        copy.start()
        sends.append(copy)

    for target in (up, dn, xp):
        send_block(t, target, vis_ref.at[rows_here, :])
    w_out = rcopy(
        wkv_hbm, wk.at[:, pl.ds(pl.multiple_of(c * 128, 128), 128)], wsend, wrecv, sib, v
    )
    w_out.start()

    def got(f):
        rcopy(vb.at[f], vb.at[f], vsend.at[0], vrecv.at[f], sib, v).wait_recv()

    acc = jnp.zeros((256, 256), F32)

    def add(acc, f):
        weights = wk[pl.ds(pl.multiple_of(f * 256, 256), 256), :]
        return acc + jnp.dot(vb[f], weights, preferred_element_type=F32)

    got(sib)
    for target in (up, dn, xp):
        send_block(sib, target)

    z_bytes = text_all.at[0, :, pl.ds(0, 15 * 128)]
    rcopy(z_bytes, z_bytes, tsend, trecv, t, vx).wait_recv()
    text_x = rcopy(text_all.at[xl], text_all.at[xl], txsend, txrecv, t, vx)
    text_x.start()

    got(xp)
    for target in (up, dn):
        send_block(xp, target)
    got(xps)
    for target in (up, dn):
        send_block(xps, target)

    up0, up1 = (col + 4) % 16, (col + 5) % 16
    dn0, dn1 = (col + 12) % 16, (col + 13) % 16
    pcol = base + (1 - xh) * 2
    pup0, pup1 = (pcol + 4) % 16, (pcol + 5) % 16
    pdn0, pdn1 = (pcol + 12) % 16, (pcol + 13) % 16
    got(dn0)
    send_block(dn0, up)
    got(up1)
    send_block(up1, dn)

    text_other = text_all.at[1 - xl]
    rcopy(text_other, text_other, txsend, txrecv, t, vx).wait_recv()
    own_wq.wait()
    q = jnp.zeros((32, 128), F32)
    for k in range(16):
        lhs = jnp.concatenate(
            [text_all[0, :, k * 128 : k * 128 + 128], text_all[1, :, k * 128 : k * 128 + 128]], axis=1
        )
        q = q + jnp.dot(lhs, wq[k * 256 : k * 256 + 256, :], preferred_element_type=F32)
    q_loc[...] = head_norm(q, qg_ref[...]).astype(BF16)
    my_rows = pl.ds(pl.multiple_of(g * 32, 32), 32)
    c1 = rcopy(q_loc, qbuf.at[j_own, my_rows, :], c1send, c1recv.at[g], t1, v)

    @pl.when(jnp.logical_not(owner))
    def _():
        c1.start()

    got(pdn0)
    send_block(pdn0, up)
    got(pup1)
    send_block(pup1, dn)

    def wo_step(zz, carry):
        src_own = wo_hbm.at[:, pl.ds(pl.multiple_of((2 * zz + xl) * 128, 128), 128)]
        src_out = wo_hbm.at[:, pl.ds(pl.multiple_of((2 * zz + 1 - xl) * 128, 128), 128)]
        dst = wo2.at[xl, :, pl.ds(pl.multiple_of(zz * 128, 128), 128)]
        pltpu.make_async_copy(src_own, dst, loc.at[3]).start()
        rcopy(src_out, dst, wosend, worecv, t, vx).start()
        return carry

    q_own = qbuf.at[j_own]

    def push_q(zz):
        rcopy(q_own, q_own, qsend, qrecv.at[j_own], t, at_z(zz)).start()

    @pl.when(owner)
    def _():
        qbuf[j_own, my_rows, :] = q_loc[...]

        def step(i, carry):
            s = lax.rem(g + i, 8)
            part = qbuf.at[j_own, pl.ds(pl.multiple_of(s * 32, 32), 32), :]
            rcopy(part, part, c1send, c1recv.at[s], t1, v).wait_recv()
            return carry

        lax.fori_loop(1, 8, step, 0)
        each_z(push_q)

    lax.fori_loop(0, 16, wo_step, 0)

    own_tokens.wait()
    own_wk.wait()
    wk_other = wk.at[:, pl.ds(pl.multiple_of((1 - c) * 128, 128), 128)]
    rcopy(wk_other, wk_other, wsend, wrecv, sib, v).wait_recv()
    acc = add(acc, t)
    acc = add(acc, sib)
    acc = add(acc, xp)
    acc = add(acc, xps)
    acc = add(acc, dn0)
    acc = add(acc, up1)
    acc = add(acc, pdn0)
    acc = add(acc, pup1)
    for f in (dn1, up0, pdn1, pup0):
        got(f)
        acc = add(acc, f)

    for jj in range(2):
        j = 2 * jj + xl

        @pl.when(v != 4 * g + j)
        def _():
            rcopy(qbuf.at[j], qbuf.at[j], qsend, qrecv.at[j], t, vx).wait_recv()

        rcopy(qbuf.at[j], qbuf.at[j], qfsend.at[jj], qrecv.at[j], t, vx).start()

    far0, far1 = (col + 8) % 16, (col + 9) % 16
    pfar0, pfar1 = (pcol + 8) % 16, (pcol + 9) % 16
    for f in (far0, far1, pfar0, pfar1):
        got(f)
        acc = add(acc, f)

    kv = acc.astype(BF16)
    raw = kv.astype(F32)
    for h in range(2):
        part = raw[:, h * 128 : h * 128 + 128]
        normed = head_norm(part, kg_ref[...])
        kvst[h] = jnp.where(half == 0, normed, part).astype(BF16)
    my_half = pl.ds(pl.multiple_of(c * 256, 256), 256)
    other_half = pl.ds(pl.multiple_of((1 - c) * 256, 256), 256)
    kv_sib = rcopy(kvst.at[1 - c], kvb.at[half, my_half, :], kvsend.at[0], kvrecv.at[0], sib, v)
    kv_far = rcopy(kvst.at[c], kvb.at[half, my_half, :], kvsend.at[1], kvrecv.at[1], far, v)
    kv_far_sib = rcopy(kvst.at[1 - c], kvb.at[half, my_half, :], kvsend.at[2], kvrecv.at[2], far_sib, v)
    kv_far.start()
    kv_far_sib.start()
    kv_sib.start()
    kvb[half, my_half, :] = kvst[c]

    for jj in range(2):
        j = 2 * jj + 1 - xl
        rcopy(qbuf.at[j], qbuf.at[j], qsend, qrecv.at[j], t, vx).wait_recv()
    rcopy(kvst.at[0], kvb.at[half, other_half, :], kvsend.at[0], kvrecv.at[0], sib, v).wait_recv()
    rcopy(kvst.at[0], kvb.at[1 - half, my_half, :], kvsend.at[1], kvrecv.at[1], far, v).wait_recv()
    rcopy(kvst.at[0], kvb.at[1 - half, other_half, :], kvsend.at[2], kvrecv.at[2], far, v).wait_recv()

    def attend(j):
        scores = lax.dot_general(
            qbuf[j], kvb[0], (((1,), (1,)), ((), ())), preferred_element_type=F32
        )
        peak = jnp.max(scores, axis=-1, keepdims=True)
        probs = jnp.exp2((scores - peak) * SCALE_LOG2)
        total = jnp.sum(probs, axis=-1, keepdims=True)
        partial = jnp.dot(probs.astype(BF16), kvb[1], preferred_element_type=F32)
        return partial, column_tile(peak * SCALE_LOG2, total)

    o_out = []
    for jj in range(2):
        partial, tile = attend(2 * jj + 1 - xl)
        o_send[jj] = partial.astype(BF16)
        t_send[jj] = tile
        copy = rcopy(o_send.at[jj], o_recv.at[jj], osend.at[jj], orecv.at[jj], t, vx)
        copy.start()
        o_out.append(copy)
        copy = rcopy(t_send.at[jj], t_recv.at[jj], ssend.at[jj], srecv.at[jj], t, vx)
        copy.start()
        o_out.append(copy)
    for jj in range(2):
        partial, tile = attend(2 * jj + xl)
        o_own[jj] = partial
        t_own[jj] = tile

    for jj in range(2):
        o_out[2 * jj].wait_recv()
        o_out[2 * jj + 1].wait_recv()
        mine, theirs = t_own[jj], t_recv[jj]
        top = jnp.maximum(mine, theirs)
        a, b = jnp.exp2(mine - top), jnp.exp2(theirs - top)
        lane = lax.broadcasted_iota(jnp.int32, (8, 128), 1)
        a = jnp.where(lane < 32, a, 0.0)
        b = jnp.where(lane < 32, b, 0.0)
        total = pltpu.roll(a, 32, 1) * mine + pltpu.roll(b, 32, 1) * theirs
        tile = jnp.where(lane < 32, top, total)
        for k in range(32):
            rows = slice(8 * k, 8 * k + 8)
            o_own[jj, rows, :] = (
                o_own[jj, rows, :] * a[:, k : k + 1]
                + o_recv[jj, rows, :].astype(F32) * b[:, k : k + 1]
            )
        o2[jj] = o_own[jj].astype(BF16)
        for rb in range(8):
            t2[jj, rb] = tile if rb == 0 else pltpu.roll(tile, 128 - 4 * rb, 1)

    def push_partial(zz):
        rows = pl.ds(pl.multiple_of((zz // 2) * 32, 32), 32)
        rcopy(o2.at[zz % 2, rows, :], d_all.at[z], dsend, drecv, t, at_z(zz)).start()
        rcopy(t2.at[zz % 2, zz // 2], t_all.at[z], t2send, t2recv, t, at_z(zz)).start()

    each_z(push_partial)
    d_all[z] = o2[z % 2, pl.ds(pl.multiple_of((z // 2) * 32, 32), 32), :]
    t_all[z] = t2[z % 2, z // 2]
    d15, t15 = d_all.at[pl.ds(0, 15)], t_all.at[pl.ds(0, 15)]
    rcopy(t15, t15, t2send, t2recv, t, vx).wait_recv()
    rcopy(d15, d15, dsend, drecv, t, vx).wait_recv()
    lane = lax.broadcasted_iota(jnp.int32, (8, 128), 1)
    top = t_all[0]
    for s in range(1, 16):
        top = jnp.maximum(top, t_all[s])
    den = jnp.zeros((8, 128), F32)
    num = [jnp.zeros((8, 128), F32) for _ in range(4)]
    for s in range(16):
        tile = t_all[s]
        w = jnp.where(lane < 4, jnp.exp2(tile - top), 0.0)
        den = den + w * pltpu.roll(tile, 96, 1)
        block = d_all[s].astype(F32)
        for k in range(4):
            num[k] = num[k] + block[8 * k : 8 * k + 8] * w[:, k : k + 1]
    attended = jnp.concatenate([num[k] / den[:, k : k + 1] for k in range(4)], axis=0)
    att[...] = attended.astype(BF16)

    a1 = rcopy(att, att_all.at[xl], asend.at[0], arecv.at[xl], t1, v1)
    a2 = rcopy(att, att_all.at[xl], asend.at[1], arecv.at[xl], t1, v2)
    a2.start()

    @pl.when(jnp.logical_not(owner))
    def _():
        a1.start()
        a1.wait_recv()

    @pl.when(owner)
    def _():
        att_all[xl] = att[...]

    a_other = att_all.at[1 - xl]
    rcopy(a_other, a_other, asend.at[1], arecv.at[1 - xl], t1, v2).wait_recv()

    pltpu.make_async_copy(wo2.at[xl], wo2.at[xl], loc.at[3]).wait()
    rcopy(wo2.at[1 - xl], wo2.at[1 - xl], wosend, worecv, t, vx).wait_recv()
    for n in range(4):
        cols = slice(n * 512, n * 512 + 512)
        terms = jnp.dot(att_all[0], wo2[0, :, cols], preferred_element_type=F32) + jnp.dot(
            att_all[1], wo2[1, :, cols], preferred_element_type=F32
        )
        for k in range(4):
            r_send[4 * n + k] = terms[:, k * 128 : k * 128 + 128].astype(BF16)

    def push_out(zz):
        rcopy(r_send.at[zz], r_recv.at[z], rsend, rrecv, t, at_z(zz)).start()

    each_z(push_out)
    r_recv[z] = r_send[z]
    r15 = r_recv.at[pl.ds(0, 15)]
    rcopy(r15, r15, rsend, rrecv, t, vx).wait_recv()
    summed = r_recv[0].astype(F32)
    for s in range(1, 16):
        summed = summed + r_recv[s].astype(F32)
    out_ref[...] = (jnp.tanh(jnp.full((32, 128), gate_ref[0], F32)) * summed).astype(BF16)

    for copy in sends:
        copy.wait_send()
    w_out.wait_send()
    rcopy(z_bytes, z_bytes, tsend, trecv, t, vx).wait_send()
    text_x.wait_send()

    @pl.when(jnp.logical_not(owner))
    def _():
        c1.wait_send()
        a1.wait_send()

    @pl.when(owner)
    def _():
        def step(i, carry):
            rcopy(q_own, q_own, qsend, qrecv.at[j_own], t, vx).wait_send()
            return carry

        lax.fori_loop(0, 15, step, 0)

    for jj in range(2):
        rcopy(qbuf.at[0], qbuf.at[0], qfsend.at[jj], qrecv.at[0], t, vx).wait_send()
    rcopy(wo2.at[xl], wo2.at[xl], wosend, worecv, t, vx).wait_send()
    for copy in (kv_sib, kv_far, kv_far_sib, a2, *o_out):
        copy.wait_send()
    rcopy(d15, d15, dsend, drecv, t, vx).wait_send()
    rcopy(t15, t15, t2send, t2recv, t, vx).wait_send()
    rcopy(r15, r15, rsend, rrecv, t, vx).wait_send()


def on_device(
    text_rows, visual, norm_gain, q_weight, key_value_weight, q_gain, k_gain, out_weight, attn_gate
):
    vmem = pl.BlockSpec(memory_space=pltpu.VMEM)
    hbm = pl.BlockSpec(memory_space=pl.ANY)
    smem = pl.BlockSpec(memory_space=pltpu.SMEM)
    dma = pltpu.SemaphoreType.DMA
    one = dma(())
    buffers = [
        pltpu.VMEM(shape, dtype)
        for shape, dtype in (
            ((32, 128), BF16),
            ((2, 32, 2048), BF16),
            ((4096, 128), BF16),
            ((4096, 256), BF16),
            ((16, 256, 256), BF16),
            ((32, 128), BF16),
            ((4, 256, 128), BF16),
            ((2, 256, 128), BF16),
            ((2, 512, 128), BF16),
            ((2, 256, 128), BF16),
            ((2, 8, 128), F32),
            ((2, 256, 128), F32),
            ((2, 8, 128), F32),
            ((2, 256, 128), BF16),
            ((2, 8, 128), F32),
            ((2, 256, 128), BF16),
            ((2, 8, 8, 128), F32),
            ((16, 32, 128), BF16),
            ((16, 8, 128), F32),
            ((32, 128), BF16),
            ((2, 32, 128), BF16),
            ((2, 128, 2048), BF16),
            ((16, 32, 128), BF16),
            ((16, 32, 128), BF16),
        )
    ]
    semaphores = [
        dma((4,)),
        dma((15,)), dma((16,)),
        one, one,
        one, one, one, one,
        one, dma((8,)),
        one, dma((2,)), dma((4,)),
        one, one,
        dma((3,)), dma((3,)),
        dma((2,)), dma((2,)), dma((2,)), dma((2,)),
        one, one, one, one,
        dma((2,)), dma((2,)),
        one, one,
    ]
    return pl.pallas_call(
        kernel,
        out_shape=jax.ShapeDtypeStruct((32, 128), BF16),
        in_specs=[vmem, hbm, vmem, hbm, hbm, vmem, vmem, hbm, smem],
        out_specs=vmem,
        scratch_shapes=buffers + semaphores,
        compiler_params=pltpu.CompilerParams(
            collective_id=0, has_side_effects=True, vmem_limit_bytes=48 * 1024 * 1024
        ),
    )(
        text_rows, visual, norm_gain.reshape(1, -1), q_weight, key_value_weight,
        q_gain.reshape(1, -1), k_gain.reshape(1, -1), out_weight, attn_gate,
    )


def solution(mesh):
    placed = (
        P("text", "vis"),
        P("vis", "text"),
        P(),
        P(None, "vis"),
        P(None, "text"),
        P(),
        P(),
        P("vis", None),
        P(),
    )
    return jax.shard_map(
        on_device, mesh=mesh, in_specs=placed, out_specs=P("text", "vis"), check_vma=False
    )
```

```python
import jax
import jax.numpy as jnp
from jax import lax
from jax.experimental import pallas as pl
from jax.experimental.pallas import tpu as pltpu
from jax.sharding import PartitionSpec as P

HEAD = 128
EPS = 1e-05
SCALE_LOG2 = (HEAD ** -0.5) * 1.4426950408889634
MESH = pl.DeviceIdType.MESH
BF16 = jnp.bfloat16
F32 = jnp.float32


def rcopy(src, dst, send, recv, t, v):
    return pltpu.make_async_remote_copy(
        src_ref=src, dst_ref=dst, send_sem=send, recv_sem=recv, device_id=(t, v), device_id_type=MESH
    )


def head_norm(heads, gain):
    mean_square = jnp.mean(heads * heads, axis=-1, keepdims=True)
    return heads * lax.rsqrt(mean_square + EPS) * gain


def column_tile(m, l):
    lane = lax.broadcasted_iota(jnp.int32, (8, 128), 1)
    tile = jnp.zeros((8, 128), F32)
    for k in range(32):
        tile = jnp.where(lane == k, m[8 * k : 8 * k + 8], tile)
        tile = jnp.where(lane == 32 + k, l[8 * k : 8 * k + 8], tile)
    return tile


def kernel(
    text_hbm, vis_ref, gain_hbm, wq_hbm, wkv_hbm, qg_hbm, kg_hbm, wo_hbm, gate_hbm,
    out_ref,
    text_ref, gain_ref, qg_ref, kg_ref, gate_ref,
    text_s, text_all, wq, wk, vb, q_loc, q_heads, qbuf, kvst, kvb,
    o_send, t_send, o_own, t_own, o_recv, t_recv, o2, t2, d_all, t_all,
    att, att_all, wo2, r_send, r_recv,
    loc, vsend, vrecv, wsend, wrecv, tsend, trecv, txsend, txrecv,
    qzsend, qzrecv, qsend, qrecv, wosend, worecv, kvsend, kvrecv, osend, orecv, ssend, srecv,
    dsend, drecv, t2send, t2recv, asend, arecv, rsend, rrecv,
):
    t = lax.axis_index("text")
    v = lax.axis_index("vis")
    z = v // 2
    xl = v % 2
    c = t % 2
    half = t // 8
    g = t % 8
    vx = 2 * z + 1 - xl
    sib = t + 1 - 2 * c
    xh = (t // 2) % 2
    base = (t // 4) * 4
    xp = base + (1 - xh) * 2 + c
    xps = base + (1 - xh) * 2 + 1 - c
    up = (t + 4) % 16
    dn = (t + 12) % 16
    far = (t + 8) % 16
    col = t - c
    far_sib = (sib + 8) % 16
    cross = jnp.where((t // 4) % 2 == 0, dn, up)
    group = half * 8
    t1 = half * 8 + v // 4
    v1 = g * 4 + v % 4
    v2 = g * 4 + (v % 4) + 1 - 2 * (v % 2)
    owner = g == v // 4

    def at_z(zz):
        return 2 * zz + xl

    def ring(i):
        return lax.rem(z + 8 + jnp.where(i % 2 == 0, -(i // 2), (i + 1) // 2), 16)

    def each_z(body):
        def step(i, carry):
            body(ring(i))
            return carry

        lax.fori_loop(0, 15, step, 0)

    own_tokens = pltpu.make_async_copy(vis_ref.at[pl.ds(c * 256, 256), :], vb.at[t], loc.at[0])
    own_wq = pltpu.make_async_copy(wq_hbm, wq, loc.at[1])
    own_wk = pltpu.make_async_copy(wkv_hbm, wk.at[:, pl.ds(pl.multiple_of(c * 128, 128), 128)], loc.at[2])
    small = [
        pltpu.make_async_copy(text_hbm, text_ref, loc.at[4]),
        pltpu.make_async_copy(
            gain_hbm.at[:, pl.ds(pl.multiple_of(v * 128, 128), 128)], gain_ref, loc.at[5]
        ),
        pltpu.make_async_copy(qg_hbm, qg_ref, loc.at[6]),
        pltpu.make_async_copy(kg_hbm, kg_ref, loc.at[7]),
        pltpu.make_async_copy(gate_hbm, gate_ref, loc.at[8]),
    ]
    for copy in small:
        copy.start()
    own_tokens.start()
    own_wk.start()
    own_wq.start()
    barrier = pltpu.get_barrier_semaphore()

    def greet(tt, vv):
        pl.semaphore_signal(barrier, inc=1, device_id=(tt, vv), device_id_type=MESH)

    def greet_group(i, carry):
        other = group + lax.rem(g + i, 8)
        greet(other, v)
        greet(other, vx)
        return carry

    for other in (far, far_sib, cross):
        greet(other, v)
    greet(t, vx)
    lax.fori_loop(1, 8, greet_group, 0)
    each_z(lambda zz: greet(t, at_z(zz)))

    @pl.when(jnp.logical_not(owner))
    def _():
        greet(t1, v1)
        greet(t1, v2)

    for copy in small:
        copy.wait()
    text_s[...] = (text_ref[...].astype(F32) * gain_ref[...]).astype(BF16)
    my_cols = pl.ds(pl.multiple_of(z * 128, 128), 128)
    text_all[xl, :, my_cols] = text_s[...]
    pl.semaphore_wait(barrier, 3 + 1 + 14 + 15 + jnp.where(owner, 0, 2))

    rows_here = pl.ds(c * 256, 256)
    rows_sib = pl.ds((1 - c) * 256, 256)
    to_sib = rcopy(vis_ref.at[rows_sib, :], vb.at[t], vsend.at[0], vrecv.at[t], sib, v)
    to_sib.start()

    def push_text(zz):
        rcopy(text_s, text_all.at[xl, :, my_cols], tsend, trecv, t, at_z(zz)).start()

    each_z(push_text)
    sends = [to_sib]

    def send_block(f, target, src=None):
        copy = rcopy(
            vb.at[f] if src is None else src, vb.at[f], vsend.at[len(sends)], vrecv.at[f], target, v
        )
        copy.start()
        sends.append(copy)

    for target in (up, dn, xp):
        send_block(t, target, vis_ref.at[rows_here, :])
    w_out = rcopy(
        wkv_hbm, wk.at[:, pl.ds(pl.multiple_of(c * 128, 128), 128)], wsend, wrecv, sib, v
    )
    w_out.start()

    def got(f):
        rcopy(vb.at[f], vb.at[f], vsend.at[0], vrecv.at[f], sib, v).wait_recv()

    acc = jnp.zeros((256, 256), F32)

    def add(acc, f):
        weights = wk[pl.ds(pl.multiple_of(f * 256, 256), 256), :]
        return acc + jnp.dot(vb[f], weights, preferred_element_type=F32)

    got(sib)
    for target in (up, dn, xp):
        send_block(sib, target)

    up0, up1 = (col + 4) % 16, (col + 5) % 16
    dn0, dn1 = (col + 12) % 16, (col + 13) % 16
    pcol = base + (1 - xh) * 2
    pup0, pup1 = (pcol + 4) % 16, (pcol + 5) % 16
    pdn0, pdn1 = (pcol + 12) % 16, (pcol + 13) % 16

    def relay(f, target):
        got(f)
        send_block(f, target)

    relay(dn0, up)
    relay(up1, dn)
    relay(pcol, up)
    relay(pcol + 1, dn)

    z_bytes = text_all.at[0, :, pl.ds(0, 15 * 128)]
    rcopy(z_bytes, z_bytes, tsend, trecv, t, vx).wait_recv()
    text_x = rcopy(text_all.at[xl], text_all.at[xl], txsend, txrecv, t, vx)
    text_x.start()

    relay(dn1, xp)
    relay(up0, xp)

    text_other = text_all.at[1 - xl]
    rcopy(text_other, text_other, txsend, txrecv, t, vx).wait_recv()
    own_wq.wait()
    q = jnp.zeros((32, 128), F32)
    for k in range(16):
        lhs = jnp.concatenate(
            [text_all[0, :, k * 128 : k * 128 + 128], text_all[1, :, k * 128 : k * 128 + 128]], axis=1
        )
        q = q + jnp.dot(lhs, wq[k * 256 : k * 256 + 256, :], preferred_element_type=F32)
    q_loc[...] = head_norm(q, qg_ref[...]).astype(BF16)
    q_heads[z] = q_loc[...]

    def push_q(zz):
        rcopy(q_loc, q_heads.at[z], qzsend, qzrecv, t, at_z(zz)).start()

    each_z(push_q)

    relay(pdn0, up)
    relay(pup1, dn)

    def wo_step(zz, carry):
        src_own = wo_hbm.at[:, pl.ds(pl.multiple_of((2 * zz + xl) * 128, 128), 128)]
        src_out = wo_hbm.at[:, pl.ds(pl.multiple_of((2 * zz + 1 - xl) * 128, 128), 128)]
        dst = wo2.at[xl, :, pl.ds(pl.multiple_of(zz * 128, 128), 128)]
        pltpu.make_async_copy(src_own, dst, loc.at[3]).start()
        rcopy(src_out, dst, wosend, worecv, t, vx).start()
        return carry

    lax.fori_loop(0, 16, wo_step, 0)

    own_tokens.wait()
    own_wk.wait()
    wk_other = wk.at[:, pl.ds(pl.multiple_of((1 - c) * 128, 128), 128)]
    rcopy(wk_other, wk_other, wsend, wrecv, sib, v).wait_recv()
    acc = add(acc, t)
    acc = add(acc, sib)
    for f in (pcol, pcol + 1, dn0, up1, dn1, up0, pdn0, pup1):
        acc = add(acc, f)

    q15 = q_heads.at[pl.ds(0, 15)]
    rcopy(q15, q15, qzsend, qzrecv, t, vx).wait_recv()

    def share_heads(i, carry):
        other = lax.rem(g + i, 8)
        part = q_heads.at[pl.ds(2 * other, 2)]
        rcopy(part, qbuf.at[xl, g], qsend, qrecv.at[xl], group + other, v).start()
        rcopy(part, qbuf.at[xl, g], qsend, qrecv.at[xl], group + other, vx).start()
        return carry

    lax.fori_loop(1, 8, share_heads, 0)
    rcopy(q_heads.at[pl.ds(2 * g, 2)], qbuf.at[xl, g], qsend, qrecv.at[xl], t, vx).start()
    qbuf[xl, g] = q_heads[pl.ds(2 * g, 2)]

    far0, far1 = (col + 8) % 16, (col + 9) % 16
    pfar0, pfar1 = (pcol + 8) % 16, (pcol + 9) % 16
    for f in (pdn1, pup0, far0, far1, pfar0, pfar1):
        got(f)
        acc = add(acc, f)

    kv = acc.astype(BF16)
    raw = kv.astype(F32)
    for h in range(2):
        part = raw[:, h * 128 : h * 128 + 128]
        normed = head_norm(part, kg_ref[...])
        kvst[h] = jnp.where(half == 0, normed, part).astype(BF16)
    my_half = pl.ds(pl.multiple_of(c * 256, 256), 256)
    other_half = pl.ds(pl.multiple_of((1 - c) * 256, 256), 256)
    kv_sib = rcopy(kvst.at[1 - c], kvb.at[half, my_half, :], kvsend.at[0], kvrecv.at[0], sib, v)
    kv_far = rcopy(kvst.at[c], kvb.at[half, my_half, :], kvsend.at[1], kvrecv.at[1], far, v)
    kv_far_sib = rcopy(kvst.at[1 - c], kvb.at[half, my_half, :], kvsend.at[2], kvrecv.at[2], far_sib, v)
    kv_far.start()
    kv_far_sib.start()
    kv_sib.start()
    kvb[half, my_half, :] = kvst[c]

    q7 = qbuf.at[xl, pl.ds(0, 7)]
    rcopy(q7, q7, qsend, qrecv.at[xl], t, vx).wait_recv()
    q8 = qbuf.at[1 - xl]
    rcopy(q8, q8, qsend, qrecv.at[1 - xl], t, vx).wait_recv()
    rcopy(kvst.at[0], kvb.at[half, other_half, :], kvsend.at[0], kvrecv.at[0], sib, v).wait_recv()
    rcopy(kvst.at[0], kvb.at[1 - half, my_half, :], kvsend.at[1], kvrecv.at[1], far, v).wait_recv()
    rcopy(kvst.at[0], kvb.at[1 - half, other_half, :], kvsend.at[2], kvrecv.at[2], far, v).wait_recv()

    def attend(parity, jj):
        queries = qbuf[parity, :, jj].reshape(256, 128)
        scores = lax.dot_general(
            queries, kvb[0], (((1,), (1,)), ((), ())), preferred_element_type=F32
        )
        peak = jnp.max(scores, axis=-1, keepdims=True)
        probs = jnp.exp2((scores - peak) * SCALE_LOG2)
        total = jnp.sum(probs, axis=-1, keepdims=True)
        partial = jnp.dot(probs.astype(BF16), kvb[1], preferred_element_type=F32)
        return partial, column_tile(peak * SCALE_LOG2, total)

    o_out = []
    for jj in range(2):
        partial, tile = attend(1 - xl, jj)
        o_send[jj] = partial.astype(BF16)
        t_send[jj] = tile
        copy = rcopy(o_send.at[jj], o_recv.at[jj], osend.at[jj], orecv.at[jj], t, vx)
        copy.start()
        o_out.append(copy)
        copy = rcopy(t_send.at[jj], t_recv.at[jj], ssend.at[jj], srecv.at[jj], t, vx)
        copy.start()
        o_out.append(copy)
    for jj in range(2):
        partial, tile = attend(xl, jj)
        o_own[jj] = partial
        t_own[jj] = tile

    for jj in range(2):
        o_out[2 * jj].wait_recv()
        o_out[2 * jj + 1].wait_recv()
        mine, theirs = t_own[jj], t_recv[jj]
        top = jnp.maximum(mine, theirs)
        a, b = jnp.exp2(mine - top), jnp.exp2(theirs - top)
        lane = lax.broadcasted_iota(jnp.int32, (8, 128), 1)
        a = jnp.where(lane < 32, a, 0.0)
        b = jnp.where(lane < 32, b, 0.0)
        total = pltpu.roll(a, 32, 1) * mine + pltpu.roll(b, 32, 1) * theirs
        tile = jnp.where(lane < 32, top, total)
        for k in range(32):
            rows = slice(8 * k, 8 * k + 8)
            o_own[jj, rows, :] = (
                o_own[jj, rows, :] * a[:, k : k + 1]
                + o_recv[jj, rows, :].astype(F32) * b[:, k : k + 1]
            )
        o2[jj] = o_own[jj].astype(BF16)
        for rb in range(8):
            t2[jj, rb] = tile if rb == 0 else pltpu.roll(tile, 128 - 4 * rb, 1)

    def push_partial(zz):
        rows = pl.ds(pl.multiple_of((zz // 2) * 32, 32), 32)
        rcopy(o2.at[zz % 2, rows, :], d_all.at[z], dsend, drecv, t, at_z(zz)).start()
        rcopy(t2.at[zz % 2, zz // 2], t_all.at[z], t2send, t2recv, t, at_z(zz)).start()

    each_z(push_partial)
    d_all[z] = o2[z % 2, pl.ds(pl.multiple_of((z // 2) * 32, 32), 32), :]
    t_all[z] = t2[z % 2, z // 2]
    d15, t15 = d_all.at[pl.ds(0, 15)], t_all.at[pl.ds(0, 15)]
    rcopy(t15, t15, t2send, t2recv, t, vx).wait_recv()
    rcopy(d15, d15, dsend, drecv, t, vx).wait_recv()
    lane = lax.broadcasted_iota(jnp.int32, (8, 128), 1)
    top = t_all[0]
    for s in range(1, 16):
        top = jnp.maximum(top, t_all[s])
    den = jnp.zeros((8, 128), F32)
    num = [jnp.zeros((8, 128), F32) for _ in range(4)]
    for s in range(16):
        tile = t_all[s]
        w = jnp.where(lane < 4, jnp.exp2(tile - top), 0.0)
        den = den + w * pltpu.roll(tile, 96, 1)
        block = d_all[s].astype(F32)
        for k in range(4):
            num[k] = num[k] + block[8 * k : 8 * k + 8] * w[:, k : k + 1]
    attended = jnp.concatenate([num[k] / den[:, k : k + 1] for k in range(4)], axis=0)
    att[...] = attended.astype(BF16)

    a1 = rcopy(att, att_all.at[xl], asend.at[0], arecv.at[xl], t1, v1)
    a2 = rcopy(att, att_all.at[xl], asend.at[1], arecv.at[xl], t1, v2)
    a2.start()

    @pl.when(jnp.logical_not(owner))
    def _():
        a1.start()
        a1.wait_recv()

    @pl.when(owner)
    def _():
        att_all[xl] = att[...]

    a_other = att_all.at[1 - xl]
    rcopy(a_other, a_other, asend.at[1], arecv.at[1 - xl], t1, v2).wait_recv()

    pltpu.make_async_copy(wo2.at[xl], wo2.at[xl], loc.at[3]).wait()
    rcopy(wo2.at[1 - xl], wo2.at[1 - xl], wosend, worecv, t, vx).wait_recv()
    for n in range(4):
        cols = slice(n * 512, n * 512 + 512)
        terms = jnp.dot(att_all[0], wo2[0, :, cols], preferred_element_type=F32) + jnp.dot(
            att_all[1], wo2[1, :, cols], preferred_element_type=F32
        )
        for k in range(4):
            r_send[4 * n + k] = terms[:, k * 128 : k * 128 + 128].astype(BF16)

    def push_out(zz):
        rcopy(r_send.at[zz], r_recv.at[z], rsend, rrecv, t, at_z(zz)).start()

    each_z(push_out)
    r_recv[z] = r_send[z]
    r15 = r_recv.at[pl.ds(0, 15)]
    rcopy(r15, r15, rsend, rrecv, t, vx).wait_recv()
    summed = r_recv[0].astype(F32)
    for s in range(1, 16):
        summed = summed + r_recv[s].astype(F32)
    out_ref[...] = (jnp.tanh(gate_ref[...]) * summed).astype(BF16)

    for copy in sends:
        copy.wait_send()
    w_out.wait_send()
    rcopy(z_bytes, z_bytes, tsend, trecv, t, vx).wait_send()
    text_x.wait_send()

    @pl.when(jnp.logical_not(owner))
    def _():
        a1.wait_send()

    rcopy(q15, q15, qzsend, qzrecv, t, vx).wait_send()
    rcopy(q7, q7, qsend, qrecv.at[xl], t, vx).wait_send()
    rcopy(q8, q8, qsend, qrecv.at[xl], t, vx).wait_send()
    rcopy(wo2.at[xl], wo2.at[xl], wosend, worecv, t, vx).wait_send()
    for copy in (kv_sib, kv_far, kv_far_sib, a2, *o_out):
        copy.wait_send()
    rcopy(d15, d15, dsend, drecv, t, vx).wait_send()
    rcopy(t15, t15, t2send, t2recv, t, vx).wait_send()
    rcopy(r15, r15, rsend, rrecv, t, vx).wait_send()


def on_device(
    text_rows, visual, norm_gain, q_weight, key_value_weight, q_gain, k_gain, out_weight, attn_gate
):
    vmem = pl.BlockSpec(memory_space=pltpu.VMEM)
    hbm = pl.BlockSpec(memory_space=pl.ANY)
    dma = pltpu.SemaphoreType.DMA
    one = dma(())
    buffers = [
        pltpu.VMEM(*buffer)
        for buffer in (
            ((32, 128), BF16),
            ((1, 128), F32),
            ((1, 128), F32),
            ((1, 128), F32),
            ((1, 1), F32),
            ((32, 128), BF16),
            ((2, 32, 2048), BF16),
            ((4096, 128), BF16),
            ((4096, 256), BF16),
            ((16, 256, 256), BF16),
            ((32, 128), BF16),
            ((16, 32, 128), BF16),
            ((2, 8, 2, 32, 128), BF16),
            ((2, 256, 128), BF16),
            ((2, 512, 128), BF16),
            ((2, 256, 128), BF16),
            ((2, 8, 128), F32),
            ((2, 256, 128), F32),
            ((2, 8, 128), F32),
            ((2, 256, 128), BF16),
            ((2, 8, 128), F32),
            ((2, 256, 128), BF16),
            ((2, 8, 8, 128), F32),
            ((16, 32, 128), BF16),
            ((16, 8, 128), F32),
            ((32, 128), BF16),
            ((2, 32, 128), BF16),
            ((2, 128, 2048), BF16),
            ((16, 32, 128), BF16),
            ((16, 32, 128), BF16),
        )
    ]
    semaphores = [
        dma((9,)),
        dma((15,)), dma((16,)),
        one, one,
        one, one, one, one,
        one, one, one, dma((2,)),
        one, one,
        dma((3,)), dma((3,)),
        dma((2,)), dma((2,)), dma((2,)), dma((2,)),
        one, one, one, one,
        dma((2,)), dma((2,)),
        one, one,
    ]
    return pl.pallas_call(
        kernel,
        out_shape=jax.ShapeDtypeStruct((32, 128), BF16),
        in_specs=[hbm] * 9,
        out_specs=vmem,
        scratch_shapes=buffers + semaphores,
        compiler_params=pltpu.CompilerParams(
            collective_id=0, has_side_effects=True, vmem_limit_bytes=60 * 1024 * 1024
        ),
    )(
        text_rows, visual, norm_gain.reshape(1, -1), q_weight, key_value_weight,
        q_gain.reshape(1, -1), k_gain.reshape(1, -1), out_weight, attn_gate.reshape(1, 1),
    )


def solution(mesh):
    placed = (
        P("text", "vis"),
        P("vis", "text"),
        P(),
        P(None, "vis"),
        P(None, "text"),
        P(),
        P(),
        P("vis", None),
        P(),
    )
    return jax.shard_map(
        on_device, mesh=mesh, in_specs=placed, out_specs=P("text", "vis"), check_vma=False
    )
```

```python
import jax
import jax.numpy as jnp
from jax import lax
from jax.experimental import pallas as pl
from jax.experimental.pallas import tpu as pltpu
from jax.sharding import PartitionSpec as P

HEAD = 128
EPS = 1e-05
SCALE_LOG2 = (HEAD ** -0.5) * 1.4426950408889634
MESH = pl.DeviceIdType.MESH
BF16 = jnp.bfloat16
F32 = jnp.float32


def rcopy(src, dst, send, recv, t, v):
    return pltpu.make_async_remote_copy(
        src_ref=src, dst_ref=dst, send_sem=send, recv_sem=recv, device_id=(t, v), device_id_type=MESH
    )


def head_norm(heads, gain):
    mean_square = jnp.mean(heads * heads, axis=-1, keepdims=True)
    return heads * lax.rsqrt(mean_square + EPS) * gain


def column_tile(columns):
    lane = lax.broadcasted_iota(jnp.int32, (8, 128), 1)
    tile = jnp.zeros((8, 128), F32)
    for i, column in enumerate(columns):
        for k in range(32):
            tile = jnp.where(lane == 32 * i + k, column[8 * k : 8 * k + 8], tile)
    return tile


def kernel(
    text_hbm, vis_ref, gain_hbm, wq_hbm, wkv_hbm, qg_hbm, kg_hbm, wo_hbm, gate_hbm,
    out_ref,
    text_ref, gain_ref, qg_ref, kg_ref, gate_ref,
    text_s, text_all, wq, wk, vb, q_loc, q_heads, qbuf, kvst, kvb,
    o_send, t_send, o_recv, t_recv, o2, t2, d_all, t_all, att, att_all, wo_all,
    loc, vsend, vrecv, wsend, wrecv, tsend, trecv, txsend, txrecv,
    qzsend, qzrecv, qsend, qrecv, kvsend, kvrecv, osend, orecv, ssend, srecv,
    dsend, drecv, t2send, t2recv, asend, arecv, axsend, axrecv,
    wzsend, wzrecv, wpsend, wprecv, wssend, wsrecv,
):
    t = lax.axis_index("text")
    v = lax.axis_index("vis")
    z = v // 2
    xl = v % 2
    c = t % 2
    half = t // 8
    g = t % 8
    vx = 2 * z + 1 - xl
    sib = t + 1 - 2 * c
    xh = (t // 2) % 2
    base = (t // 4) * 4
    xp = base + (1 - xh) * 2 + c
    up = (t + 4) % 16
    dn = (t + 12) % 16
    far = (t + 8) % 16
    col = t - c
    pcol = base + (1 - xh) * 2
    far_sib = (sib + 8) % 16
    cross = jnp.where((t // 4) % 2 == 0, dn, up)
    group = half * 8
    own_half = half == 0

    def at_z(zz):
        return 2 * zz + xl

    def each_z(body):
        def step(i, carry):
            body(lax.rem(z + 8 + jnp.where(i % 2 == 0, -(i // 2), (i + 1) // 2), 16), i)
            return carry

        lax.fori_loop(0, 15, step, 0)

    def lanes(i):
        return pl.ds(pl.multiple_of(i * 128, 128), 128)

    small = [
        pltpu.make_async_copy(text_hbm, text_ref, loc.at[4]),
        pltpu.make_async_copy(gain_hbm.at[:, lanes(v)], gain_ref, loc.at[5]),
        pltpu.make_async_copy(qg_hbm, qg_ref, loc.at[6]),
        pltpu.make_async_copy(kg_hbm, kg_ref, loc.at[7]),
        pltpu.make_async_copy(gate_hbm, gate_ref, loc.at[8]),
    ]
    for copy in small:
        copy.start()
    own_tokens = pltpu.make_async_copy(vis_ref.at[pl.ds(c * 256, 256), :], vb.at[t], loc.at[0])
    own_wq = pltpu.make_async_copy(wq_hbm, wq, loc.at[1])
    own_wk = pltpu.make_async_copy(wkv_hbm, wk.at[:, lanes(c)], loc.at[2])
    own_tokens.start()
    own_wk.start()
    own_wq.start()

    barrier = pltpu.get_barrier_semaphore()

    def greet(tt, vv):
        pl.semaphore_signal(barrier, inc=1, device_id=(tt, vv), device_id_type=MESH)

    def greet_group(i, carry):
        other = group + lax.rem(g + i, 8)
        greet(other, v)
        greet(other, vx)
        return carry

    for other in (far, far_sib, cross):
        greet(other, v)
    greet(t, vx)
    lax.fori_loop(1, 8, greet_group, 0)
    each_z(lambda zz, i: greet(t, at_z(zz)))

    @pl.when(c == 1)
    def _():
        each_z(lambda zz, i: greet(t, 2 * zz + 1 - xl))

    for copy in small:
        copy.wait()
    text_s[...] = (text_ref[...].astype(F32) * gain_ref[...]).astype(BF16)
    text_all[xl, :, lanes(z)] = text_s[...]
    pl.semaphore_wait(barrier, 3 + 1 + 14 + 15 + 15 * c)

    def push_columns(block, everything, send, recv):
        def push(zz, i):
            near = jnp.where(i < 7, 1, 0)
            rcopy(block, everything.at[xl, :, lanes(z)], send, recv.at[near], t, at_z(zz)).start()

        each_z(push)

    def forward_columns(everything, recv, xsend, xrecv, far_group):
        count = 7 if far_group else 8
        part = everything.at[0, :, pl.ds(0, count * 128)]
        rcopy(part, part, xsend, recv.at[far_group], t, vx).wait_recv()

        def forward(i, carry):
            mine = everything.at[xl, :, lanes(lax.rem(z + i, 16))]
            rcopy(mine, mine, xsend, xrecv, t, vx).start()
            return carry

        lax.fori_loop(*((5, 12) if far_group else (12, 21)), forward, 0)

    push_columns(text_s, text_all, tsend, trecv)

    sends = []

    def piece(f, h):
        return vb.at[f, pl.ds(h * 128, 128), :]

    def send_block(f, h, target, src=None):
        copy = rcopy(
            piece(f, h) if src is None else src, piece(f, h),
            vsend.at[len(sends)], vrecv.at[f + 16 * h], target, v,
        )
        copy.start()
        sends.append(copy)

    def got(f, h):
        rcopy(piece(f, h), piece(f, h), vsend.at[0], vrecv.at[f + 16 * h], sib, v).wait_recv()

    def relay(f, h, *targets):
        got(f, h)
        for target in targets:
            send_block(f, h, target)

    for h in range(2):
        send_block(t, h, sib, vis_ref.at[pl.ds((1 - c) * 256 + h * 128, 128), :])
        for target in (up, dn, xp):
            send_block(t, h, target, vis_ref.at[pl.ds(c * 256 + h * 128, 128), :])
    w_out = rcopy(wkv_hbm, wk.at[:, lanes(c)], wsend, wrecv, sib, v)
    w_out.start()
    for h in range(2):
        relay(sib, h, up, dn, xp)

    up0, up1 = (col + 4) % 16, (col + 5) % 16
    dn0, dn1 = (col + 12) % 16, (col + 13) % 16
    far0, far1 = (col + 8) % 16, (col + 9) % 16
    pup0, pup1 = (pcol + 4) % 16, (pcol + 5) % 16
    pdn0, pdn1 = (pcol + 12) % 16, (pcol + 13) % 16
    pfar0, pfar1 = (pcol + 8) % 16, (pcol + 9) % 16

    def relays_first(h):
        relay(dn0, h, up)
        relay(up1, h, dn)
        relay(pcol, h, up)
        relay(pcol + 1, h, dn)

    def relays_second(h):
        relay(dn1, h, xp)
        relay(up0, h, xp)
        relay(pdn0, h, up)
        relay(pup1, h, dn)

    forward_columns(text_all, trecv, txsend, txrecv, 0)
    relays_first(0)
    forward_columns(text_all, trecv, txsend, txrecv, 1)
    relays_second(0)

    text_other = text_all.at[1 - xl]
    rcopy(text_other, text_other, txsend, txrecv, t, vx).wait_recv()
    own_wq.wait()
    q = jnp.zeros((32, 128), F32)
    for k in range(16):
        lhs = jnp.concatenate(
            [text_all[0, :, k * 128 : k * 128 + 128], text_all[1, :, k * 128 : k * 128 + 128]], axis=1
        )
        q = q + jnp.dot(lhs, wq[k * 256 : k * 256 + 256, :], preferred_element_type=F32)
    q_loc[...] = head_norm(q, qg_ref[...]).astype(BF16)
    q_heads[z] = q_loc[...]
    each_z(
        lambda zz, i: rcopy(
            q_loc, q_heads.at[z], qzsend, qzrecv.at[z], t, at_z(zz)
        ).start()
    )

    w_rows = pl.ds(pl.multiple_of((t // 2) * 16, 16), 16)
    qw = (xl + c) % 2

    def push_w(zz):
        rcopy(
            wo_hbm.at[w_rows, lanes(2 * zz + qw)], wo_all.at[xl, z, w_rows, :],
            wzsend, wzrecv, t, 2 * zz + qw,
        ).start()

    own_w = pltpu.make_async_copy(
        wo_hbm.at[w_rows, lanes(v)], wo_all.at[xl, z, w_rows, :], loc.at[3]
    )
    each_z(lambda zz, i: push_w(zz))

    @pl.when(c == 0)
    def _():
        own_w.start()

    @pl.when(c == 1)
    def _():
        push_w(z)

    relays_first(1)
    relays_second(1)

    def share_heads(i, carry):
        other = lax.rem(z // 2 + 8 + jnp.where(i % 2 == 0, -(i // 2), (i + 1) // 2), 8)
        for e in range(2):
            zz = 2 * other + e

            @pl.when(zz != z)
            def _():
                rcopy(q_loc, q_heads.at[zz], qzsend, qzrecv.at[zz], t, vx).wait_recv()

        part = q_heads.at[pl.ds(2 * other, 2)]
        rcopy(part, qbuf.at[xl, g], qsend, qrecv.at[xl], group + other, vx).start()

        @pl.when(other != g)
        def _():
            rcopy(part, qbuf.at[xl, g], qsend, qrecv.at[xl], group + other, v).start()

        @pl.when(other == g)
        def _():
            qbuf[xl, g] = q_heads[pl.ds(2 * g, 2)]

        return carry

    lax.fori_loop(0, 4, share_heads, 0)

    own_tokens.wait()
    own_wk.wait()
    wk_other = wk.at[:, lanes(1 - c)]
    rcopy(wk_other, wk_other, wsend, wrecv, sib, v).wait_recv()
    kv_sends = []

    def project(h):
        for f in (pdn1, pup0, far0, far1, pfar0, pfar1):
            got(f, h)
        acc = jnp.zeros((128, 256), F32)
        for f in range(16):
            acc = acc + jnp.dot(
                vb[f, h * 128 : h * 128 + 128, :], wk[f * 256 : f * 256 + 256, :],
                preferred_element_type=F32,
            )
        raw = acc.astype(BF16).astype(F32)
        for n in range(2):
            part = raw[:, n * 128 : n * 128 + 128]
            normed = head_norm(part, kg_ref[...])
            kvst[h, n] = jnp.where(own_half, normed, part).astype(BF16)
        rows = pl.ds(pl.multiple_of(c * 256 + h * 128, 128), 128)
        for i, (n, target) in enumerate(((c, far), (1 - c, far_sib), (1 - c, sib))):
            copy = rcopy(
                kvst.at[h, n], kvb.at[half, rows, :], kvsend.at[3 * h + i], kvrecv.at[3 * h + i], target, v
            )
            copy.start()
            kv_sends.append(copy)
        kvb[half, rows, :] = kvst[h, c]

    project(0)
    lax.fori_loop(4, 8, share_heads, 0)
    project(1)

    def w_block(f):
        return wo_all.at[qw, :, pl.ds(pl.multiple_of((f // 2) * 16, 16), 16), :]

    w_sends = []

    def w_send(f, *targets):
        for target in targets:
            copy = rcopy(w_block(f), w_block(f), wpsend.at[len(w_sends)], wprecv.at[f // 2], target, v)
            copy.start()
            w_sends.append(copy)

    def w_got(f):
        rcopy(w_block(f), w_block(f), wpsend.at[0], wprecv.at[f // 2], sib, v).wait_recv()

    def w_landed(count):
        return wo_all.at[qw, pl.ds(0, count), pl.ds(0, 16), :]

    @pl.when(c == 0)
    def _():
        own_w.wait()
        rcopy(w_landed(15), w_landed(15), wzsend, wzrecv, t, vx).wait_recv()

    @pl.when(c == 1)
    def _():
        rcopy(w_landed(16), w_landed(16), wzsend, wzrecv, t, vx).wait_recv()

    w_send(t, xp, up, dn)

    q7 = qbuf.at[xl, pl.ds(0, 7)]
    rcopy(q7, q7, qsend, qrecv.at[xl], t, vx).wait_recv()
    q8 = qbuf.at[1 - xl]
    rcopy(q8, q8, qsend, qrecv.at[1 - xl], t, vx).wait_recv()
    for h in range(2):
        here = pl.ds(pl.multiple_of(c * 256 + h * 128, 128), 128)
        there = pl.ds(pl.multiple_of((1 - c) * 256 + h * 128, 128), 128)
        for i, rows in ((0, (1 - half, here)), (1, (1 - half, there)), (2, (half, there))):
            block = kvb.at[rows[0], rows[1], :]
            rcopy(block, block, kvsend.at[0], kvrecv.at[3 * h + i], sib, v).wait_recv()

    def attend(parity):
        columns = []
        for jj in range(2):
            scores = lax.dot_general(
                qbuf[parity, :, jj].reshape(256, 128), kvb[0], (((1,), (1,)), ((), ())),
                preferred_element_type=F32,
            )
            peak = jnp.max(scores, axis=-1, keepdims=True)
            probs = jnp.exp2((scores - peak) * SCALE_LOG2)
            columns += [peak * SCALE_LOG2, jnp.sum(probs, axis=-1, keepdims=True)]
            partial = jnp.dot(probs.astype(BF16), kvb[1], preferred_element_type=F32)
            o_send[parity, :, jj] = partial.astype(BF16).reshape(8, 32, 128)
        t_send[parity] = column_tile(columns)

    def send_partial(parity, rb, vv):
        rcopy(
            o_send.at[parity, rb], o_recv.at[xl, g], osend, orecv.at[xl, g], group + rb, vv
        ).start()
        rcopy(
            t_send.at[parity], t_recv.at[xl, g], ssend, srecv.at[xl, g], group + rb, vv
        ).start()

    def send_other(i, carry):
        send_partial(1 - xl, lax.rem(g + i, 8), vx)
        return carry

    def send_own(i, carry):
        send_partial(xl, lax.rem(g + i, 8), v)
        return carry

    attend(1 - xl)
    lax.fori_loop(0, 8, send_other, 0)
    attend(xl)
    lax.fori_loop(1, 8, send_own, 0)
    o_recv[xl, g] = o_send[xl, g]
    t_recv[xl, g] = t_send[xl]

    w_got(xp)
    w_send(xp, up, dn)
    w_got(dn)
    w_send(dn, up)

    lane = lax.broadcasted_iota(jnp.int32, (8, 128), 1)
    sub = lax.broadcasted_iota(jnp.int32, (8, 128), 0)

    def merge(i, carry):
        src = lax.rem(g + i, 8)
        for x in range(2):

            @pl.when(jnp.logical_or(x != xl, src != g))
            def _():
                rcopy(o_recv.at[x, src], o_recv.at[x, src], osend, orecv.at[x, src], t, vx).wait_recv()
                rcopy(t_recv.at[x, src], t_recv.at[x, src], ssend, srecv.at[x, src], t, vx).wait_recv()

        shift = lax.rem(128 - 4 * g, 128)
        first = pltpu.roll(t_recv[0, src], shift, 1)
        second = pltpu.roll(t_recv[1, src], shift, 1)
        top = jnp.maximum(first, second)
        a = jnp.exp2(first - top)
        b = jnp.exp2(second - top)
        total = pltpu.roll(a, 32, 1) * first + pltpu.roll(b, 32, 1) * second
        for jj in range(2):
            zz = 2 * src + jj
            row = jnp.zeros((8, 128), F32)
            blocks = []
            for k in range(4):
                m, l = 64 * jj + k, 64 * jj + 32 + k
                row = jnp.where(lane == 8 * sub + k, top[:, m : m + 1], row)
                row = jnp.where(lane == 8 * sub + 4 + k, total[:, l : l + 1], row)
                rows = slice(8 * k, 8 * k + 8)
                blocks.append(
                    o_recv[0, src, jj].astype(F32)[rows] * a[:, m : m + 1]
                    + o_recv[1, src, jj].astype(F32)[rows] * b[:, m : m + 1]
                )
            o2[zz] = jnp.concatenate(blocks, axis=0).astype(BF16)
            t2[zz, 0:1, :] = jnp.sum(row, axis=0, keepdims=True)

            @pl.when(zz != z)
            def _():
                rcopy(o2.at[zz], d_all.at[z], dsend, drecv, t, at_z(zz)).start()
                rcopy(
                    t2.at[zz, pl.ds(0, 1), :], t_all.at[z, pl.ds(0, 1), :], t2send, t2recv, t, at_z(zz)
                ).start()

            @pl.when(zz == z)
            def _():
                d_all[z] = o2[zz]
                t_all[z, 0:1, :] = t2[zz, 0:1, :]

        return carry

    lax.fori_loop(0, 8, merge, 0)

    w_got(far)
    w_send(far, xp)

    d15, t15 = d_all.at[pl.ds(0, 15)], t_all.at[pl.ds(0, 15), pl.ds(0, 1), :]
    rcopy(t15, t15, t2send, t2recv, t, vx).wait_recv()
    rcopy(d15, d15, dsend, drecv, t, vx).wait_recv()
    top = t_all[0, 0:1, :]
    for s in range(1, 16):
        top = jnp.maximum(top, t_all[s, 0:1, :])

    def column(row, k):
        return jnp.sum(
            jnp.where(lane == 8 * sub + k, jnp.broadcast_to(row, (8, 128)), 0.0), axis=1, keepdims=True
        )

    den = jnp.zeros((1, 128), F32)
    num = [jnp.zeros((8, 128), F32) for _ in range(4)]
    for s in range(16):
        row = t_all[s, 0:1, :]
        w = jnp.exp2(row - top)
        den = den + w * pltpu.roll(row, 124, 1)
        block = d_all[s].astype(F32)
        for k in range(4):
            num[k] = num[k] + block[8 * k : 8 * k + 8] * column(w, k)
    attended = jnp.concatenate([num[k] / column(den, k) for k in range(4)], axis=0)
    att[...] = attended.astype(BF16)
    att_all[xl, :, lanes(z)] = att[...]
    push_columns(att, att_all, asend, arecv)

    for f in (up, pup0, pdn0, pfar0):
        w_got(f)
    w_sib = rcopy(wo_all.at[qw], wo_all.at[qw], wssend, wsrecv, sib, v)
    w_sib.start()

    forward_columns(att_all, arecv, axsend, axrecv, 0)
    forward_columns(att_all, arecv, axsend, axrecv, 1)
    rcopy(wo_all.at[1 - qw], wo_all.at[1 - qw], wssend, wsrecv, sib, v).wait_recv()
    att_other = att_all.at[1 - xl]
    rcopy(att_other, att_other, axsend, axrecv, t, vx).wait_recv()
    summed = jnp.zeros((32, 128), F32)
    for n in range(2):
        for k in range(8):
            summed = summed + jnp.dot(
                att_all[n, :, k * 256 : k * 256 + 256],
                wo_all[n, 2 * k : 2 * k + 2].reshape(256, 128),
                preferred_element_type=F32,
            )
    out_ref[...] = (jnp.tanh(gate_ref[...]) * summed).astype(BF16)

    for copy in (*sends, w_out, *kv_sends, *w_sends, w_sib):
        copy.wait_send()
    for everything, send, xsend in ((text_all, tsend, txsend), (att_all, asend, axsend)):
        block = everything.at[0, :, pl.ds(0, 15 * 128)]
        rcopy(block, block, send, trecv.at[0], t, vx).wait_send()
        rcopy(everything.at[0], everything.at[0], xsend, trecv.at[0], t, vx).wait_send()
    q15 = q_heads.at[pl.ds(0, 15)]
    rcopy(q15, q15, qzsend, qzrecv.at[0], t, vx).wait_send()
    rcopy(q7, q7, qsend, qrecv.at[xl], t, vx).wait_send()
    rcopy(q8, q8, qsend, qrecv.at[xl], t, vx).wait_send()
    o15 = o_recv.at[0, pl.ds(0, 7)]
    rcopy(o15, o15, osend, orecv.at[0, 0], t, vx).wait_send()
    rcopy(o_recv.at[0], o_recv.at[0], osend, orecv.at[0, 0], t, vx).wait_send()
    s15 = t_recv.at[0, pl.ds(0, 7)]
    rcopy(s15, s15, ssend, srecv.at[0, 0], t, vx).wait_send()
    rcopy(t_recv.at[0], t_recv.at[0], ssend, srecv.at[0, 0], t, vx).wait_send()
    rcopy(d15, d15, dsend, drecv, t, vx).wait_send()
    rcopy(t15, t15, t2send, t2recv, t, vx).wait_send()

    @pl.when(c == 0)
    def _():
        rcopy(w_landed(15), w_landed(15), wzsend, wzrecv, t, vx).wait_send()

    @pl.when(c == 1)
    def _():
        rcopy(w_landed(16), w_landed(16), wzsend, wzrecv, t, vx).wait_send()


def on_device(
    text_rows, visual, norm_gain, q_weight, key_value_weight, q_gain, k_gain, out_weight, attn_gate
):
    vmem = pl.BlockSpec(memory_space=pltpu.VMEM)
    hbm = pl.BlockSpec(memory_space=pl.ANY)
    dma = pltpu.SemaphoreType.DMA
    one = dma(())
    buffers = [
        pltpu.VMEM(*buffer)
        for buffer in (
            ((32, 128), BF16),
            ((1, 128), F32),
            ((1, 128), F32),
            ((1, 128), F32),
            ((1, 1), F32),
            ((32, 128), BF16),
            ((2, 32, 2048), BF16),
            ((4096, 128), BF16),
            ((4096, 256), BF16),
            ((16, 256, 256), BF16),
            ((32, 128), BF16),
            ((16, 32, 128), BF16),
            ((2, 8, 2, 32, 128), BF16),
            ((2, 2, 128, 128), BF16),
            ((2, 512, 128), BF16),
            ((2, 8, 2, 32, 128), BF16),
            ((2, 8, 128), F32),
            ((2, 8, 2, 32, 128), BF16),
            ((2, 8, 8, 128), F32),
            ((16, 32, 128), BF16),
            ((16, 8, 128), F32),
            ((16, 32, 128), BF16),
            ((16, 8, 128), F32),
            ((32, 128), BF16),
            ((2, 32, 2048), BF16),
            ((2, 16, 128, 128), BF16),
        )
    ]
    semaphores = [
        dma((9,)),
        dma((30,)), dma((32,)),
        one, one,
        one, dma((2,)), one, one,
        one, dma((16,)), one, dma((2,)),
        dma((6,)), dma((6,)),
        one, dma((2, 8)), one, dma((2, 8)),
        one, one, one, one,
        one, dma((2,)), one, one,
        one, one, dma((7,)), dma((8,)), one, one,
    ]
    return pl.pallas_call(
        kernel,
        out_shape=jax.ShapeDtypeStruct((32, 128), BF16),
        in_specs=[hbm] * 9,
        out_specs=vmem,
        scratch_shapes=buffers + semaphores,
        compiler_params=pltpu.CompilerParams(
            collective_id=0, has_side_effects=True, vmem_limit_bytes=60 * 1024 * 1024
        ),
    )(
        text_rows, visual, norm_gain.reshape(1, -1), q_weight, key_value_weight,
        q_gain.reshape(1, -1), k_gain.reshape(1, -1), out_weight, attn_gate.reshape(1, 1),
    )


def solution(mesh):
    placed = (
        P("text", "vis"),
        P("vis", "text"),
        P(),
        P(None, "vis"),
        P(None, "text"),
        P(),
        P(),
        P("vis", None),
        P(),
    )
    return jax.shard_map(
        on_device, mesh=mesh, in_specs=placed, out_specs=P("text", "vis"), check_vma=False
    )
```

```python
import jax
import jax.numpy as jnp
from jax import lax
from jax.experimental import pallas as pl
from jax.experimental.pallas import tpu as pltpu
from jax.sharding import PartitionSpec as P

HEAD = 128
EPS = 1e-05
SCALE_LOG2 = (HEAD ** -0.5) * 1.4426950408889634
MESH = pl.DeviceIdType.MESH
BF16 = jnp.bfloat16
F32 = jnp.float32


def rcopy(src, dst, send, recv, t, v):
    return pltpu.make_async_remote_copy(
        src_ref=src, dst_ref=dst, send_sem=send, recv_sem=recv, device_id=(t, v), device_id_type=MESH
    )


def head_norm(heads, gain):
    mean_square = jnp.mean(heads * heads, axis=-1, keepdims=True)
    return heads * lax.rsqrt(mean_square + EPS) * gain


def column_tile(columns):
    lane = lax.broadcasted_iota(jnp.int32, (8, 128), 1)
    tile = jnp.zeros((8, 128), F32)
    for i, column in enumerate(columns):
        for k in range(32):
            tile = jnp.where(lane == 32 * i + k, column[8 * k : 8 * k + 8], tile)
    return tile


def kernel(
    text_hbm, vis_ref, gain_hbm, wq_hbm, wkv_hbm, qg_hbm, kg_hbm, wo_hbm, gate_hbm,
    out_ref,
    text_ref, gain_ref, qg_ref, kg_ref, gate_ref,
    text_s, text_all, wq, wk, vb, q_loc, q_heads, qbuf, kvst, kvb,
    o_send, t_send, o_recv, t_recv, o2, t2, d_all, t_all, att, att_all, wo_all, terms_send, terms_recv,
    loc, vsend, vrecv, wsend, wrecv, tsend, trecv, txsend, txrecv,
    qzsend, qzrecv, qsend, qrecv, kvsend, kvrecv, osend, orecv, ssend, srecv,
    dsend, drecv, t2send, t2recv, asend, arecv, axsend, axrecv,
    wzsend, wzrecv, wpsend, wprecv, wssend, wsrecv,
):
    t = lax.axis_index("text")
    v = lax.axis_index("vis")
    z = v // 2
    xl = v % 2
    c = t % 2
    half = t // 8
    g = t % 8
    vx = 2 * z + 1 - xl
    sib = t + 1 - 2 * c
    xh = (t // 2) % 2
    base = (t // 4) * 4
    xp = base + (1 - xh) * 2 + c
    up = (t + 4) % 16
    dn = (t + 12) % 16
    far = (t + 8) % 16
    col = t - c
    pcol = base + (1 - xh) * 2
    far_sib = (sib + 8) % 16
    cross = jnp.where((t // 4) % 2 == 0, dn, up)
    group = half * 8
    own_half = half == 0

    def at_z(zz):
        return 2 * zz + xl

    def each_z(body):
        def step(i, carry):
            body(lax.rem(z + 8 + jnp.where(i % 2 == 0, -(i // 2), (i + 1) // 2), 16), i)
            return carry

        lax.fori_loop(0, 15, step, 0)

    def nearest(i):
        bits = [(g // n % 2 + i // n % 2) % 2 for n in (1, 2, 4)]
        return bits[0] + 2 * bits[1] + 4 * bits[2]

    def lanes(i):
        return pl.ds(pl.multiple_of(i * 128, 128), 128)

    barrier = pltpu.get_barrier_semaphore()

    def greet(tt, vv):
        pl.semaphore_signal(barrier, inc=1, device_id=(tt, vv), device_id_type=MESH)

    def greet_group(i, carry):
        other = group + lax.rem(g + i, 8)
        greet(other, v)
        greet(other, vx)
        return carry

    each_z(lambda zz, i: greet(t, at_z(zz)))
    for other in (far, far_sib, cross):
        greet(other, v)
    lax.fori_loop(1, 8, greet_group, 0)
    greet(t, vx)

    small = [
        pltpu.make_async_copy(text_hbm, text_ref, loc.at[4]),
        pltpu.make_async_copy(gain_hbm.at[:, lanes(v)], gain_ref, loc.at[5]),
        pltpu.make_async_copy(qg_hbm, qg_ref, loc.at[6]),
        pltpu.make_async_copy(kg_hbm, kg_ref, loc.at[7]),
        pltpu.make_async_copy(gate_hbm, gate_ref, loc.at[8]),
    ]
    for copy in small:
        copy.start()
    own_tokens = pltpu.make_async_copy(vis_ref.at[pl.ds(c * 256, 256), :], vb.at[t], loc.at[0])
    own_wq = pltpu.make_async_copy(wq_hbm, wq, loc.at[1])
    own_wk = pltpu.make_async_copy(wkv_hbm, wk.at[:, lanes(c)], loc.at[2])
    own_tokens.start()
    own_wk.start()
    own_wq.start()

    for copy in small:
        copy.wait()
    text_s[...] = (text_ref[...].astype(F32) * gain_ref[...]).astype(BF16)
    text_all[xl, :, lanes(z)] = text_s[...]
    pl.semaphore_wait(barrier, 15 + 3 + 14 + 1)

    groups = ((10, 23),), ((7, 10),)

    def push_text(zz, i):
        stage = jnp.where(i < 3, 1, 0)
        rcopy(text_s, text_all.at[xl, :, lanes(z)], tsend, trecv.at[stage], t, at_z(zz)).start()

    each_z(push_text)

    def forward_text(stage):
        part = text_all.at[0, :, pl.ds(0, (12, 3)[stage] * 128)]
        rcopy(part, part, txsend, trecv.at[stage], t, vx).wait_recv()

        def forward(i, carry):
            mine = text_all.at[xl, :, lanes(lax.rem(z + i, 16))]
            rcopy(mine, mine, txsend, txrecv, t, vx).start()
            return carry

        for first, last in groups[stage]:
            lax.fori_loop(first, last, forward, 0)

    sends = []

    def piece(f, h):
        return vb.at[f, pl.ds(h * 128, 128), :]

    def send_block(f, h, target, src=None):
        copy = rcopy(
            piece(f, h) if src is None else src, piece(f, h),
            vsend.at[len(sends)], vrecv.at[f + 16 * h], target, v,
        )
        copy.start()
        sends.append(copy)

    def got(f, h):
        rcopy(piece(f, h), piece(f, h), vsend.at[0], vrecv.at[f + 16 * h], sib, v).wait_recv()

    def relay(f, h, *targets):
        got(f, h)
        for target in targets:
            send_block(f, h, target)

    for h in range(2):
        send_block(t, h, sib, vis_ref.at[pl.ds((1 - c) * 256 + h * 128, 128), :])
        for target in (up, dn, xp):
            send_block(t, h, target, vis_ref.at[pl.ds(c * 256 + h * 128, 128), :])
    w_out = rcopy(wkv_hbm, wk.at[:, lanes(c)], wsend, wrecv, sib, v)
    w_out.start()
    for h in range(2):
        relay(sib, h, up, dn, xp)

    up0, up1 = (col + 4) % 16, (col + 5) % 16
    dn0, dn1 = (col + 12) % 16, (col + 13) % 16
    far0, far1 = (col + 8) % 16, (col + 9) % 16
    pup0, pup1 = (pcol + 4) % 16, (pcol + 5) % 16
    pdn0, pdn1 = (pcol + 12) % 16, (pcol + 13) % 16
    pfar0, pfar1 = (pcol + 8) % 16, (pcol + 9) % 16

    def relays_first(h):
        relay(dn0, h, up)
        relay(up1, h, dn)
        relay(pcol, h, up)
        relay(pcol + 1, h, dn)

    def relays_second(h):
        relay(dn1, h, xp)
        relay(up0, h, xp)
        relay(pdn0, h, up)
        relay(pup1, h, dn)

    relays_first(0)
    forward_text(0)
    relays_first(1)
    forward_text(1)

    text_other = text_all.at[1 - xl]
    rcopy(text_other, text_other, txsend, txrecv, t, vx).wait_recv()
    own_wq.wait()
    q = jnp.zeros((32, 128), F32)
    for k in range(16):
        lhs = jnp.concatenate(
            [text_all[0, :, k * 128 : k * 128 + 128], text_all[1, :, k * 128 : k * 128 + 128]], axis=1
        )
        q = q + jnp.dot(lhs, wq[k * 256 : k * 256 + 256, :], preferred_element_type=F32)
    q_loc[...] = head_norm(q, qg_ref[...]).astype(BF16)
    q_heads[z] = q_loc[...]
    each_z(
        lambda zz, i: rcopy(
            q_loc, q_heads.at[z], qzsend, qzrecv.at[z], t, at_z(zz)
        ).start()
    )

    w_rows = pl.ds(pl.multiple_of((t // 2) * 16, 16), 16)
    own_w = pltpu.make_async_copy(
        wo_hbm.at[w_rows, lanes(2 * z + c)], wo_all.at[c, z, w_rows, :], loc.at[3]
    )
    own_w.start()
    each_z(
        lambda zz, i: rcopy(
            wo_hbm.at[w_rows, lanes(2 * zz + c)], wo_all.at[c, z, w_rows, :],
            wzsend, wzrecv, t, at_z(zz),
        ).start()
    )

    for h in range(2):
        relays_second(h)

    def share_heads(i, carry):
        other = lax.rem(z // 2 + 8 + jnp.where(i % 2 == 0, -(i // 2), (i + 1) // 2), 8)
        for e in range(2):
            zz = 2 * other + e

            @pl.when(zz != z)
            def _():
                rcopy(q_loc, q_heads.at[zz], qzsend, qzrecv.at[zz], t, vx).wait_recv()

        part = q_heads.at[pl.ds(2 * other, 2)]
        rcopy(part, qbuf.at[xl, g], qsend, qrecv.at[xl], group + other, vx).start()

        @pl.when(other != g)
        def _():
            rcopy(part, qbuf.at[xl, g], qsend, qrecv.at[xl], group + other, v).start()

        @pl.when(other == g)
        def _():
            qbuf[xl, g] = q_heads[pl.ds(2 * g, 2)]

        return carry

    lax.fori_loop(0, 4, share_heads, 0)

    own_tokens.wait()
    own_wk.wait()
    wk_other = wk.at[:, lanes(1 - c)]
    rcopy(wk_other, wk_other, wsend, wrecv, sib, v).wait_recv()
    kv_sends = []

    def project(h):
        for f in (pdn1, pup0, far0, far1, pfar0, pfar1):
            got(f, h)
        acc = jnp.zeros((128, 256), F32)
        for f in range(16):
            acc = acc + jnp.dot(
                vb[f, h * 128 : h * 128 + 128, :], wk[f * 256 : f * 256 + 256, :],
                preferred_element_type=F32,
            )
        raw = acc.astype(BF16).astype(F32)
        for n in range(2):
            part = raw[:, n * 128 : n * 128 + 128]
            normed = head_norm(part, kg_ref[...])
            kvst[h, n] = jnp.where(own_half, normed, part).astype(BF16)
        rows = pl.ds(pl.multiple_of(c * 256 + h * 128, 128), 128)
        for i, (n, target) in enumerate(((c, far), (1 - c, far_sib), (1 - c, sib))):
            copy = rcopy(
                kvst.at[h, n], kvb.at[half, rows, :], kvsend.at[3 * h + i], kvrecv.at[3 * h + i], target, v
            )
            copy.start()
            kv_sends.append(copy)
        kvb[half, rows, :] = kvst[h, c]

    project(0)
    lax.fori_loop(4, 8, share_heads, 0)
    project(1)

    def w_block(f):
        return wo_all.at[c, :, pl.ds(pl.multiple_of((f // 2) * 16, 16), 16), :]

    w_sends = []

    def w_send(f, *targets):
        for target in targets:
            copy = rcopy(w_block(f), w_block(f), wpsend.at[len(w_sends)], wprecv.at[f // 2], target, v)
            copy.start()
            w_sends.append(copy)

    def w_got(f):
        rcopy(w_block(f), w_block(f), wpsend.at[0], wprecv.at[f // 2], sib, v).wait_recv()

    w_landed = wo_all.at[c, pl.ds(0, 15), pl.ds(0, 16), :]
    own_w.wait()
    rcopy(w_landed, w_landed, wzsend, wzrecv, t, vx).wait_recv()
    w_send(t, xp, up, dn)

    q7 = qbuf.at[xl, pl.ds(0, 7)]
    rcopy(q7, q7, qsend, qrecv.at[xl], t, vx).wait_recv()
    q8 = qbuf.at[1 - xl]
    rcopy(q8, q8, qsend, qrecv.at[1 - xl], t, vx).wait_recv()
    for h in range(2):
        here = pl.ds(pl.multiple_of(c * 256 + h * 128, 128), 128)
        there = pl.ds(pl.multiple_of((1 - c) * 256 + h * 128, 128), 128)
        for i, rows in ((0, (1 - half, here)), (1, (1 - half, there)), (2, (half, there))):
            block = kvb.at[rows[0], rows[1], :]
            rcopy(block, block, kvsend.at[0], kvrecv.at[3 * h + i], sib, v).wait_recv()

    def attend(parity):
        columns = []
        for jj in range(2):
            scores = lax.dot_general(
                qbuf[parity, :, jj].reshape(256, 128), kvb[0], (((1,), (1,)), ((), ())),
                preferred_element_type=F32,
            )
            peak = jnp.max(scores, axis=-1, keepdims=True)
            probs = jnp.exp2((scores - peak) * SCALE_LOG2)
            columns += [peak * SCALE_LOG2, jnp.sum(probs, axis=-1, keepdims=True)]
            partial = jnp.dot(probs.astype(BF16), kvb[1], preferred_element_type=F32)
            o_send[parity, :, jj] = partial.astype(BF16).reshape(8, 32, 128)
        t_send[parity] = column_tile(columns)

    def send_partial(parity, rb, vv):
        rcopy(
            o_send.at[parity, rb], o_recv.at[xl, g], osend, orecv.at[xl, g], group + rb, vv
        ).start()
        rcopy(
            t_send.at[parity], t_recv.at[xl, g], ssend, srecv.at[xl, g], group + rb, vv
        ).start()

    def send_other(i, carry):
        send_partial(1 - xl, nearest(7 - i), vx)
        return carry

    def send_own(i, carry):
        send_partial(xl, nearest(8 - i), v)
        return carry

    attend(1 - xl)
    lax.fori_loop(0, 8, send_other, 0)
    attend(xl)
    lax.fori_loop(1, 8, send_own, 0)
    o_recv[xl, g] = o_send[xl, g]
    t_recv[xl, g] = t_send[xl]

    w_got(xp)
    w_send(xp, up, dn)
    w_got(dn)
    w_send(dn, up)

    lane = lax.broadcasted_iota(jnp.int32, (8, 128), 1)
    sub = lax.broadcasted_iota(jnp.int32, (8, 128), 0)

    def merge(i, carry):
        src = nearest(i)
        for x in range(2):

            @pl.when(jnp.logical_or(x != xl, src != g))
            def _():
                rcopy(o_recv.at[x, src], o_recv.at[x, src], osend, orecv.at[x, src], t, vx).wait_recv()
                rcopy(t_recv.at[x, src], t_recv.at[x, src], ssend, srecv.at[x, src], t, vx).wait_recv()

        shift = lax.rem(128 - 4 * g, 128)
        first = pltpu.roll(t_recv[0, src], shift, 1)
        second = pltpu.roll(t_recv[1, src], shift, 1)
        top = jnp.maximum(first, second)
        a = jnp.exp2(first - top)
        b = jnp.exp2(second - top)
        total = pltpu.roll(a, 32, 1) * first + pltpu.roll(b, 32, 1) * second
        for jj in range(2):
            zz = 2 * src + jj
            row = jnp.zeros((8, 128), F32)
            blocks = []
            for k in range(4):
                m, l = 64 * jj + k, 64 * jj + 32 + k
                row = jnp.where(lane == 8 * sub + k, top[:, m : m + 1], row)
                row = jnp.where(lane == 8 * sub + 4 + k, total[:, l : l + 1], row)
                rows = slice(8 * k, 8 * k + 8)
                blocks.append(
                    o_recv[0, src, jj].astype(F32)[rows] * a[:, m : m + 1]
                    + o_recv[1, src, jj].astype(F32)[rows] * b[:, m : m + 1]
                )
            o2[zz] = jnp.concatenate(blocks, axis=0).astype(BF16)
            t2[zz, 0:1, :] = jnp.sum(row, axis=0, keepdims=True)

            @pl.when(zz != z)
            def _():
                rcopy(o2.at[zz], d_all.at[z], dsend, drecv, t, at_z(zz)).start()
                rcopy(
                    t2.at[zz, pl.ds(0, 1), :], t_all.at[z, pl.ds(0, 1), :], t2send, t2recv, t, at_z(zz)
                ).start()

            @pl.when(zz == z)
            def _():
                d_all[z] = o2[zz]
                t_all[z, 0:1, :] = t2[zz, 0:1, :]

        return carry

    lax.fori_loop(0, 8, merge, 0)

    w_got(far)
    w_send(far, xp)

    for copy in (*sends, w_out, *kv_sends, *w_sends):
        copy.wait_send()
    z15 = att_all.at[:, pl.ds(0, 15 * 128)]
    rcopy(z15, z15, tsend, trecv.at[0], t, vx).wait_send()
    rcopy(text_all.at[0], text_all.at[0], txsend, txrecv, t, vx).wait_send()
    q15 = q_heads.at[pl.ds(0, 15)]
    rcopy(q15, q15, qzsend, qzrecv.at[0], t, vx).wait_send()
    for blocks in (q7, q8):
        rcopy(blocks, blocks, qsend, qrecv.at[xl], t, vx).wait_send()
    rcopy(w_landed, w_landed, wzsend, wzrecv, t, vx).wait_send()
    for blocks in (o_recv.at[0], o_recv.at[0, pl.ds(0, 7)]):
        rcopy(blocks, blocks, osend, orecv.at[0, 0], t, vx).wait_send()
    for blocks in (t_recv.at[0], t_recv.at[0, pl.ds(0, 7)]):
        rcopy(blocks, blocks, ssend, srecv.at[0, 0], t, vx).wait_send()

    d15, t15 = d_all.at[pl.ds(0, 15)], t_all.at[pl.ds(0, 15), pl.ds(0, 1), :]
    rcopy(t15, t15, t2send, t2recv, t, vx).wait_recv()
    rcopy(d15, d15, dsend, drecv, t, vx).wait_recv()
    top = t_all[0, 0:1, :]
    for s in range(1, 16):
        top = jnp.maximum(top, t_all[s, 0:1, :])

    def column(row, k):
        return jnp.sum(
            jnp.where(lane == 8 * sub + k, jnp.broadcast_to(row, (8, 128)), 0.0), axis=1, keepdims=True
        )

    den = jnp.zeros((1, 128), F32)
    num = [jnp.zeros((8, 128), F32) for _ in range(4)]
    for s in range(16):
        row = t_all[s, 0:1, :]
        w = jnp.exp2(row - top)
        den = den + w * pltpu.roll(row, 124, 1)
        block = d_all[s].astype(F32)
        for k in range(4):
            num[k] = num[k] + block[8 * k : 8 * k + 8] * column(w, k)
    attended = jnp.concatenate([num[k] / column(den, k) for k in range(4)], axis=0)
    att[...] = attended.astype(BF16)
    att_all[:, lanes(z)] = att[...]
    each_z(
        lambda zz, i: rcopy(att, att_all.at[:, lanes(z)], asend, arecv, t, at_z(zz)).start()
    )

    for f in (up, pup0, pdn0, pfar0):
        w_got(f)
    w_sib = rcopy(wo_all.at[c], wo_all.at[c], wssend, wsrecv, sib, v)
    w_sib.start()

    rcopy(wo_all.at[1 - c], wo_all.at[1 - c], wssend, wsrecv, sib, v).wait_recv()

    rcopy(z15, z15, asend, arecv, t, vx).wait_recv()

    def project_out(parity):
        terms = jnp.zeros((32, 128), F32)
        for k in range(8):
            terms = terms + jnp.dot(
                att_all[:, k * 256 : k * 256 + 256],
                wo_all[parity, 2 * k : 2 * k + 2].reshape(256, 128),
                preferred_element_type=F32,
            )
        return terms

    terms_send[...] = project_out(1 - xl)
    terms_x = rcopy(terms_send, terms_recv, axsend, axrecv, t, vx)
    terms_x.start()
    mine = project_out(xl)
    terms_x.wait_recv()
    out_ref[...] = (jnp.tanh(gate_ref[...]) * (mine + terms_recv[...])).astype(BF16)
    w_sib.wait_send()
    rcopy(z15, z15, asend, arecv, t, vx).wait_send()
    terms_x.wait_send()
    rcopy(d15, d15, dsend, drecv, t, vx).wait_send()
    rcopy(t15, t15, t2send, t2recv, t, vx).wait_send()


def on_device(
    text_rows, visual, norm_gain, q_weight, key_value_weight, q_gain, k_gain, out_weight, attn_gate
):
    vmem = pl.BlockSpec(memory_space=pltpu.VMEM)
    hbm = pl.BlockSpec(memory_space=pl.ANY)
    dma = pltpu.SemaphoreType.DMA
    one = dma(())
    buffers = [
        pltpu.VMEM(*buffer)
        for buffer in (
            ((32, 128), BF16),
            ((1, 128), F32),
            ((1, 128), F32),
            ((1, 128), F32),
            ((1, 1), F32),
            ((32, 128), BF16),
            ((2, 32, 2048), BF16),
            ((4096, 128), BF16),
            ((4096, 256), BF16),
            ((16, 256, 256), BF16),
            ((32, 128), BF16),
            ((16, 32, 128), BF16),
            ((2, 8, 2, 32, 128), BF16),
            ((2, 2, 128, 128), BF16),
            ((2, 512, 128), BF16),
            ((2, 8, 2, 32, 128), BF16),
            ((2, 8, 128), F32),
            ((2, 8, 2, 32, 128), BF16),
            ((2, 8, 8, 128), F32),
            ((16, 32, 128), BF16),
            ((16, 8, 128), F32),
            ((16, 32, 128), BF16),
            ((16, 8, 128), F32),
            ((32, 128), BF16),
            ((32, 2048), BF16),
            ((2, 16, 128, 128), BF16),
            ((32, 128), F32),
            ((32, 128), F32),
        )
    ]
    semaphores = [
        dma((9,)),
        dma((30,)), dma((32,)),
        one, one,
        one, dma((2,)), one, one,
        one, dma((16,)), one, dma((2,)),
        dma((6,)), dma((6,)),
        one, dma((2, 8)), one, dma((2, 8)),
        one, one, one, one,
        one, one, one, one,
        one, one, dma((7,)), dma((8,)), one, one,
    ]
    return pl.pallas_call(
        kernel,
        out_shape=jax.ShapeDtypeStruct((32, 128), BF16),
        in_specs=[hbm] * 9,
        out_specs=vmem,
        scratch_shapes=buffers + semaphores,
        compiler_params=pltpu.CompilerParams(
            collective_id=0, has_side_effects=True, vmem_limit_bytes=60 * 1024 * 1024
        ),
    )(
        text_rows, visual, norm_gain.reshape(1, -1), q_weight, key_value_weight,
        q_gain.reshape(1, -1), k_gain.reshape(1, -1), out_weight, attn_gate.reshape(1, 1),
    )


def solution(mesh):
    placed = (
        P("text", "vis"),
        P("vis", "text"),
        P(),
        P(None, "vis"),
        P(None, "text"),
        P(),
        P(),
        P("vis", None),
        P(),
    )
    return jax.shard_map(
        on_device, mesh=mesh, in_specs=placed, out_specs=P("text", "vis"), check_vma=False
    )
```

```python
import jax
import jax.numpy as jnp
from jax import lax
from jax.experimental import pallas as pl
from jax.experimental.pallas import tpu as pltpu
from jax.sharding import PartitionSpec as P

HEAD = 128
EPS = 1e-05
SCALE_LOG2 = (HEAD ** -0.5) * 1.4426950408889634
MESH = pl.DeviceIdType.MESH
BF16 = jnp.bfloat16
F32 = jnp.float32


def rcopy(src, dst, send, recv, t, v):
    return pltpu.make_async_remote_copy(
        src_ref=src, dst_ref=dst, send_sem=send, recv_sem=recv, device_id=(t, v), device_id_type=MESH
    )


def head_norm(heads, gain):
    mean_square = jnp.mean(heads * heads, axis=-1, keepdims=True)
    return heads * lax.rsqrt(mean_square + EPS) * gain


def column_tile(columns):
    lane = lax.broadcasted_iota(jnp.int32, (8, 128), 1)
    tile = jnp.zeros((8, 128), F32)
    for i, column in enumerate(columns):
        for k in range(32):
            tile = jnp.where(lane == 32 * i + k, column[8 * k : 8 * k + 8], tile)
    return tile


def kernel(
    text_hbm, vis_ref, gain_hbm, wq_hbm, wkv_hbm, qg_hbm, kg_hbm, wo_hbm, gate_hbm,
    out_ref,
    text_ref, gain_ref, qg_ref, kg_ref, gate_ref,
    text_s, text_all, wq, wk, vb, q_loc, q_heads, qbuf, kvst, kvb,
    o_send, t_send, o_recv, t_recv, o2, t2, d_all, t_all, att, att_all, wo_all, terms_send, terms_recv,
    loc, vsend, vrecv, wsend, wrecv, tsend, trecv, txsend, txrecv,
    qzsend, qzrecv, qsend, qrecv, kvsend, kvrecv, osend, orecv, ssend, srecv,
    dsend, drecv, t2send, t2recv, asend, arecv, axsend, axrecv,
    wzsend, wzrecv, wpsend, wprecv, wssend, wsrecv,
):
    t = lax.axis_index("text")
    v = lax.axis_index("vis")
    z = v // 2
    xl = v % 2
    c = t % 2
    half = t // 8
    g = t % 8
    vx = 2 * z + 1 - xl
    sib = t + 1 - 2 * c
    xh = (t // 2) % 2
    base = (t // 4) * 4
    xp = base + (1 - xh) * 2 + c
    up = (t + 4) % 16
    dn = (t + 12) % 16
    far = (t + 8) % 16
    col = t - c
    pcol = base + (1 - xh) * 2
    far_sib = (sib + 8) % 16
    cross = jnp.where((t // 4) % 2 == 0, dn, up)
    group = half * 8
    own_half = half == 0

    def at_z(zz):
        return 2 * zz + xl

    def each_z(body):
        def step(i, carry):
            body(lax.rem(z + 8 + jnp.where(i % 2 == 0, -(i // 2), (i + 1) // 2), 16), i)
            return carry

        lax.fori_loop(0, 15, step, 0)

    def nearest(i):
        bits = [(g // n % 2 + i // n % 2) % 2 for n in (1, 2, 4)]
        return bits[0] + 2 * bits[1] + 4 * bits[2]

    def lanes(i):
        return pl.ds(pl.multiple_of(i * 128, 128), 128)

    barrier = pltpu.get_barrier_semaphore()

    def greet(tt, vv):
        pl.semaphore_signal(barrier, inc=1, device_id=(tt, vv), device_id_type=MESH)

    def greet_group(i, carry):
        other = group + lax.rem(g + i, 8)
        greet(other, v)
        greet(other, vx)
        return carry

    each_z(lambda zz, i: greet(t, at_z(zz)))
    for other in (far, far_sib, cross):
        greet(other, v)
    lax.fori_loop(1, 8, greet_group, 0)
    greet(t, vx)

    small = [
        pltpu.make_async_copy(text_hbm, text_ref, loc.at[4]),
        pltpu.make_async_copy(gain_hbm.at[:, lanes(v)], gain_ref, loc.at[5]),
        pltpu.make_async_copy(qg_hbm, qg_ref, loc.at[6]),
        pltpu.make_async_copy(kg_hbm, kg_ref, loc.at[7]),
        pltpu.make_async_copy(gate_hbm, gate_ref, loc.at[8]),
    ]
    for copy in small:
        copy.start()
    own_tokens = pltpu.make_async_copy(vis_ref.at[pl.ds(c * 256, 256), :], vb.at[t], loc.at[0])
    own_wq = pltpu.make_async_copy(wq_hbm, wq, loc.at[1])
    own_wk = pltpu.make_async_copy(wkv_hbm, wk.at[:, lanes(c)], loc.at[2])
    own_tokens.start()
    own_wk.start()
    own_wq.start()

    for copy in small:
        copy.wait()
    text_s[...] = (text_ref[...].astype(F32) * gain_ref[...]).astype(BF16)
    text_all[xl, :, lanes(z)] = text_s[...]
    pl.semaphore_wait(barrier, 15 + 3 + 14 + 1)

    groups = ((10, 23),), ((7, 10),)

    def push_text(zz, i):
        stage = jnp.where(i < 3, 1, 0)
        rcopy(text_s, text_all.at[xl, :, lanes(z)], tsend, trecv.at[stage], t, at_z(zz)).start()

    each_z(push_text)

    def forward_text(stage):
        part = text_all.at[0, :, pl.ds(0, (12, 3)[stage] * 128)]
        rcopy(part, part, txsend, trecv.at[stage], t, vx).wait_recv()

        def forward(i, carry):
            mine = text_all.at[xl, :, lanes(lax.rem(z + i, 16))]
            rcopy(mine, mine, txsend, txrecv, t, vx).start()
            return carry

        for first, last in groups[stage]:
            lax.fori_loop(first, last, forward, 0)

    sends = []

    def piece(f, h):
        return vb.at[f, pl.ds(h * 128, 128), :]

    def send_block(f, h, target, src=None):
        copy = rcopy(
            piece(f, h) if src is None else src, piece(f, h),
            vsend.at[len(sends)], vrecv.at[f + 16 * h], target, v,
        )
        copy.start()
        sends.append(copy)

    def got(f, h):
        rcopy(piece(f, h), piece(f, h), vsend.at[0], vrecv.at[f + 16 * h], sib, v).wait_recv()

    def relay(f, h, *targets):
        got(f, h)
        for target in targets:
            send_block(f, h, target)

    for h in range(2):
        send_block(t, h, sib, vis_ref.at[pl.ds((1 - c) * 256 + h * 128, 128), :])
        for target in (up, dn, xp):
            send_block(t, h, target, vis_ref.at[pl.ds(c * 256 + h * 128, 128), :])
    w_out = rcopy(wkv_hbm, wk.at[:, lanes(c)], wsend, wrecv, sib, v)
    w_out.start()
    for h in range(2):
        relay(sib, h, up, dn, xp)

    up0, up1 = (col + 4) % 16, (col + 5) % 16
    dn0, dn1 = (col + 12) % 16, (col + 13) % 16
    far0, far1 = (col + 8) % 16, (col + 9) % 16
    pup0, pup1 = (pcol + 4) % 16, (pcol + 5) % 16
    pdn0, pdn1 = (pcol + 12) % 16, (pcol + 13) % 16
    pfar0, pfar1 = (pcol + 8) % 16, (pcol + 9) % 16

    def relays_first(h):
        relay(dn0, h, up)
        relay(up1, h, dn)
        relay(pcol, h, up)
        relay(pcol + 1, h, dn)

    def relays_second(h):
        relay(dn1, h, xp)
        relay(up0, h, xp)
        relay(pdn0, h, up)
        relay(pup1, h, dn)

    relays_first(0)
    forward_text(0)
    relays_first(1)
    forward_text(1)

    text_other = text_all.at[1 - xl]
    rcopy(text_other, text_other, txsend, txrecv, t, vx).wait_recv()
    own_wq.wait()
    q = jnp.zeros((32, 128), F32)
    for k in range(16):
        lhs = jnp.concatenate(
            [text_all[0, :, k * 128 : k * 128 + 128], text_all[1, :, k * 128 : k * 128 + 128]], axis=1
        )
        q = q + jnp.dot(lhs, wq[k * 256 : k * 256 + 256, :], preferred_element_type=F32)
    q_loc[...] = head_norm(q, qg_ref[...]).astype(BF16)
    q_heads[z] = q_loc[...]
    each_z(
        lambda zz, i: rcopy(
            q_loc, q_heads.at[z], qzsend, qzrecv.at[z], t, at_z(zz)
        ).start()
    )

    w_rows = pl.ds(pl.multiple_of((t // 2) * 16, 16), 16)
    own_w = pltpu.make_async_copy(
        wo_hbm.at[w_rows, lanes(2 * z + c)], wo_all.at[c, z, w_rows, :], loc.at[3]
    )
    own_w.start()
    each_z(
        lambda zz, i: rcopy(
            wo_hbm.at[w_rows, lanes(2 * zz + c)], wo_all.at[c, z, w_rows, :],
            wzsend, wzrecv, t, at_z(zz),
        ).start()
    )

    for h in range(2):
        relays_second(h)

    def share_heads(i, carry):
        other = lax.rem(z // 2 + 6 + 4 * (i // 4) + (g + i) % 4, 8)
        for e in range(2):
            zz = 2 * other + e

            @pl.when(zz != z)
            def _():
                rcopy(q_loc, q_heads.at[zz], qzsend, qzrecv.at[zz], t, vx).wait_recv()

        part = q_heads.at[pl.ds(2 * other, 2)]
        rcopy(part, qbuf.at[xl, g], qsend, qrecv.at[xl], group + other, vx).start()

        @pl.when(other != g)
        def _():
            rcopy(part, qbuf.at[xl, g], qsend, qrecv.at[xl], group + other, v).start()

        @pl.when(other == g)
        def _():
            qbuf[xl, g] = q_heads[pl.ds(2 * g, 2)]

        return carry

    lax.fori_loop(0, 4, share_heads, 0)

    own_tokens.wait()
    own_wk.wait()
    wk_other = wk.at[:, lanes(1 - c)]
    rcopy(wk_other, wk_other, wsend, wrecv, sib, v).wait_recv()
    kv_sends = []

    def project(h):
        for f in (pdn1, pup0, far0, far1, pfar0, pfar1):
            got(f, h)
        acc = jnp.zeros((128, 256), F32)
        for f in range(16):
            acc = acc + jnp.dot(
                vb[f, h * 128 : h * 128 + 128, :], wk[f * 256 : f * 256 + 256, :],
                preferred_element_type=F32,
            )
        raw = acc.astype(BF16).astype(F32)
        for n in range(2):
            part = raw[:, n * 128 : n * 128 + 128]
            normed = head_norm(part, kg_ref[...])
            kvst[h, n] = jnp.where(own_half, normed, part).astype(BF16)
        rows = pl.ds(pl.multiple_of(c * 256 + h * 128, 128), 128)
        for i, (n, target) in enumerate(((c, far), (1 - c, far_sib), (1 - c, sib))):
            copy = rcopy(
                kvst.at[h, n], kvb.at[half, rows, :], kvsend.at[3 * h + i], kvrecv.at[3 * h + i], target, v
            )
            copy.start()
            kv_sends.append(copy)
        kvb[half, rows, :] = kvst[h, c]

    project(0)
    lax.fori_loop(4, 8, share_heads, 0)
    project(1)

    def w_block(f):
        return wo_all.at[c, :, pl.ds(pl.multiple_of((f // 2) * 16, 16), 16), :]

    w_sends = []

    def w_send(f, *targets):
        for target in targets:
            copy = rcopy(w_block(f), w_block(f), wpsend.at[len(w_sends)], wprecv.at[f // 2], target, v)
            copy.start()
            w_sends.append(copy)

    def w_got(f):
        rcopy(w_block(f), w_block(f), wpsend.at[0], wprecv.at[f // 2], sib, v).wait_recv()

    w_landed = wo_all.at[c, pl.ds(0, 15), pl.ds(0, 16), :]
    own_w.wait()
    rcopy(w_landed, w_landed, wzsend, wzrecv, t, vx).wait_recv()

    q7 = qbuf.at[xl, pl.ds(0, 7)]
    rcopy(q7, q7, qsend, qrecv.at[xl], t, vx).wait_recv()
    q8 = qbuf.at[1 - xl]
    rcopy(q8, q8, qsend, qrecv.at[1 - xl], t, vx).wait_recv()
    for h in range(2):
        here = pl.ds(pl.multiple_of(c * 256 + h * 128, 128), 128)
        there = pl.ds(pl.multiple_of((1 - c) * 256 + h * 128, 128), 128)
        for i, rows in ((0, (1 - half, here)), (1, (1 - half, there)), (2, (half, there))):
            block = kvb.at[rows[0], rows[1], :]
            rcopy(block, block, kvsend.at[0], kvrecv.at[3 * h + i], sib, v).wait_recv()

    def attend(parity):
        columns = []
        for jj in range(2):
            scores = lax.dot_general(
                qbuf[parity, :, jj].reshape(256, 128), kvb[0], (((1,), (1,)), ((), ())),
                preferred_element_type=F32,
            )
            peak = jnp.max(scores, axis=-1, keepdims=True)
            probs = jnp.exp2((scores - peak) * SCALE_LOG2)
            columns += [peak * SCALE_LOG2, jnp.sum(probs, axis=-1, keepdims=True)]
            partial = jnp.dot(probs.astype(BF16), kvb[1], preferred_element_type=F32)
            o_send[parity, :, jj] = partial.astype(BF16).reshape(8, 32, 128)
        t_send[parity] = column_tile(columns)

    def send_partial(parity, rb, vv):
        rcopy(
            o_send.at[parity, rb], o_recv.at[xl, g], osend, orecv.at[xl, g], group + rb, vv
        ).start()
        rcopy(
            t_send.at[parity], t_recv.at[xl, g], ssend, srecv.at[xl, g], group + rb, vv
        ).start()

    def send_other(i, carry):
        send_partial(1 - xl, nearest(7 - i), vx)
        return carry

    def send_own(i, carry):
        send_partial(xl, nearest(8 - i), v)
        return carry

    attend(1 - xl)
    lax.fori_loop(0, 8, send_other, 0)
    attend(xl)
    lax.fori_loop(1, 8, send_own, 0)
    o_recv[xl, g] = o_send[xl, g]
    t_recv[xl, g] = t_send[xl]

    w_send(t, xp, far, up, dn)

    lane = lax.broadcasted_iota(jnp.int32, (8, 128), 1)
    sub = lax.broadcasted_iota(jnp.int32, (8, 128), 0)

    def merge(i, carry):
        src = lax.rem(z // 2 + 8 + jnp.where(i % 2 == 0, -(i // 2), (i + 1) // 2) + 4, 8)
        for x in range(2):

            @pl.when(jnp.logical_or(x != xl, src != g))
            def _():
                rcopy(o_recv.at[x, src], o_recv.at[x, src], osend, orecv.at[x, src], t, vx).wait_recv()
                rcopy(t_recv.at[x, src], t_recv.at[x, src], ssend, srecv.at[x, src], t, vx).wait_recv()

        shift = lax.rem(128 - 4 * g, 128)
        first = pltpu.roll(t_recv[0, src], shift, 1)
        second = pltpu.roll(t_recv[1, src], shift, 1)
        top = jnp.maximum(first, second)
        a = jnp.exp2(first - top)
        b = jnp.exp2(second - top)
        total = pltpu.roll(a, 32, 1) * first + pltpu.roll(b, 32, 1) * second
        for jj in range(2):
            zz = 2 * src + jj
            row = jnp.zeros((8, 128), F32)
            blocks = []
            for k in range(4):
                m, l = 64 * jj + k, 64 * jj + 32 + k
                row = jnp.where(lane == 8 * sub + k, top[:, m : m + 1], row)
                row = jnp.where(lane == 8 * sub + 4 + k, total[:, l : l + 1], row)
                rows = slice(8 * k, 8 * k + 8)
                blocks.append(
                    o_recv[0, src, jj].astype(F32)[rows] * a[:, m : m + 1]
                    + o_recv[1, src, jj].astype(F32)[rows] * b[:, m : m + 1]
                )
            o2[zz] = jnp.concatenate(blocks, axis=0).astype(BF16)
            t2[zz, 0:1, :] = jnp.sum(row, axis=0, keepdims=True)

            @pl.when(zz != z)
            def _():
                rcopy(o2.at[zz], d_all.at[z], dsend, drecv, t, at_z(zz)).start()
                rcopy(
                    t2.at[zz, pl.ds(0, 1), :], t_all.at[z, pl.ds(0, 1), :], t2send, t2recv, t, at_z(zz)
                ).start()

            @pl.when(zz == z)
            def _():
                d_all[z] = o2[zz]
                t_all[z, 0:1, :] = t2[zz, 0:1, :]

        return carry

    lax.fori_loop(0, 8, merge, 0)

    w_got(xp)
    w_send(xp, far, up, dn)

    for copy in (*sends, w_out, *kv_sends, *w_sends):
        copy.wait_send()
    z15 = att_all.at[:, pl.ds(0, 15 * 128)]
    rcopy(z15, z15, tsend, trecv.at[0], t, vx).wait_send()
    rcopy(text_all.at[0], text_all.at[0], txsend, txrecv, t, vx).wait_send()
    q15 = q_heads.at[pl.ds(0, 15)]
    rcopy(q15, q15, qzsend, qzrecv.at[0], t, vx).wait_send()
    for blocks in (q7, q8):
        rcopy(blocks, blocks, qsend, qrecv.at[xl], t, vx).wait_send()
    rcopy(w_landed, w_landed, wzsend, wzrecv, t, vx).wait_send()
    for blocks in (o_recv.at[0], o_recv.at[0, pl.ds(0, 7)]):
        rcopy(blocks, blocks, osend, orecv.at[0, 0], t, vx).wait_send()
    for blocks in (t_recv.at[0], t_recv.at[0, pl.ds(0, 7)]):
        rcopy(blocks, blocks, ssend, srecv.at[0, 0], t, vx).wait_send()

    d15, t15 = d_all.at[pl.ds(0, 15)], t_all.at[pl.ds(0, 15), pl.ds(0, 1), :]
    rcopy(t15, t15, t2send, t2recv, t, vx).wait_recv()
    rcopy(d15, d15, dsend, drecv, t, vx).wait_recv()
    top = t_all[0, 0:1, :]
    for s in range(1, 16):
        top = jnp.maximum(top, t_all[s, 0:1, :])

    def column(row, k):
        return jnp.sum(
            jnp.where(lane == 8 * sub + k, jnp.broadcast_to(row, (8, 128)), 0.0), axis=1, keepdims=True
        )

    den = jnp.zeros((1, 128), F32)
    num = [jnp.zeros((8, 128), F32) for _ in range(4)]
    for s in range(16):
        row = t_all[s, 0:1, :]
        w = jnp.exp2(row - top)
        den = den + w * pltpu.roll(row, 124, 1)
        block = d_all[s].astype(F32)
        for k in range(4):
            num[k] = num[k] + block[8 * k : 8 * k + 8] * column(w, k)
    attended = jnp.concatenate([num[k] / column(den, k) for k in range(4)], axis=0)
    att[...] = attended.astype(BF16)
    att_all[:, lanes(z)] = att[...]
    each_z(
        lambda zz, i: rcopy(att, att_all.at[:, lanes(z)], asend, arecv, t, at_z(zz)).start()
    )

    for f in (up, dn, far, pup0, pdn0, pfar0):
        w_got(f)
    w_sib = rcopy(wo_all.at[c], wo_all.at[c], wssend, wsrecv, sib, v)
    w_sib.start()

    rcopy(wo_all.at[1 - c], wo_all.at[1 - c], wssend, wsrecv, sib, v).wait_recv()

    rcopy(z15, z15, asend, arecv, t, vx).wait_recv()

    def project_out(parity):
        terms = jnp.zeros((32, 128), F32)
        for k in range(8):
            terms = terms + jnp.dot(
                att_all[:, k * 256 : k * 256 + 256],
                wo_all[parity, 2 * k : 2 * k + 2].reshape(256, 128),
                preferred_element_type=F32,
            )
        return terms

    terms_send[...] = project_out(1 - xl)
    terms_x = rcopy(terms_send, terms_recv, axsend, axrecv, t, vx)
    terms_x.start()
    mine = project_out(xl)
    terms_x.wait_recv()
    out_ref[...] = (jnp.tanh(gate_ref[...]) * (mine + terms_recv[...])).astype(BF16)
    w_sib.wait_send()
    rcopy(z15, z15, asend, arecv, t, vx).wait_send()
    terms_x.wait_send()
    rcopy(d15, d15, dsend, drecv, t, vx).wait_send()
    rcopy(t15, t15, t2send, t2recv, t, vx).wait_send()


def on_device(
    text_rows, visual, norm_gain, q_weight, key_value_weight, q_gain, k_gain, out_weight, attn_gate
):
    vmem = pl.BlockSpec(memory_space=pltpu.VMEM)
    hbm = pl.BlockSpec(memory_space=pl.ANY)
    dma = pltpu.SemaphoreType.DMA
    one = dma(())
    buffers = [
        pltpu.VMEM(*buffer)
        for buffer in (
            ((32, 128), BF16),
            ((1, 128), F32),
            ((1, 128), F32),
            ((1, 128), F32),
            ((1, 1), F32),
            ((32, 128), BF16),
            ((2, 32, 2048), BF16),
            ((4096, 128), BF16),
            ((4096, 256), BF16),
            ((16, 256, 256), BF16),
            ((32, 128), BF16),
            ((16, 32, 128), BF16),
            ((2, 8, 2, 32, 128), BF16),
            ((2, 2, 128, 128), BF16),
            ((2, 512, 128), BF16),
            ((2, 8, 2, 32, 128), BF16),
            ((2, 8, 128), F32),
            ((2, 8, 2, 32, 128), BF16),
            ((2, 8, 8, 128), F32),
            ((16, 32, 128), BF16),
            ((16, 8, 128), F32),
            ((16, 32, 128), BF16),
            ((16, 8, 128), F32),
            ((32, 128), BF16),
            ((32, 2048), BF16),
            ((2, 16, 128, 128), BF16),
            ((32, 128), F32),
            ((32, 128), F32),
        )
    ]
    semaphores = [
        dma((9,)),
        dma((30,)), dma((32,)),
        one, one,
        one, dma((2,)), one, one,
        one, dma((16,)), one, dma((2,)),
        dma((6,)), dma((6,)),
        one, dma((2, 8)), one, dma((2, 8)),
        one, one, one, one,
        one, one, one, one,
        one, one, dma((7,)), dma((8,)), one, one,
    ]
    return pl.pallas_call(
        kernel,
        out_shape=jax.ShapeDtypeStruct((32, 128), BF16),
        in_specs=[hbm] * 9,
        out_specs=vmem,
        scratch_shapes=buffers + semaphores,
        compiler_params=pltpu.CompilerParams(
            collective_id=0, has_side_effects=True, vmem_limit_bytes=60 * 1024 * 1024
        ),
    )(
        text_rows, visual, norm_gain.reshape(1, -1), q_weight, key_value_weight,
        q_gain.reshape(1, -1), k_gain.reshape(1, -1), out_weight, attn_gate.reshape(1, 1),
    )


def solution(mesh):
    placed = (
        P("text", "vis"),
        P("vis", "text"),
        P(),
        P(None, "vis"),
        P(None, "text"),
        P(),
        P(),
        P("vis", None),
        P(),
    )
    return jax.shard_map(
        on_device, mesh=mesh, in_specs=placed, out_specs=P("text", "vis"), check_vma=False
    )
```

```python
import jax
import jax.numpy as jnp
from jax import lax
from jax.experimental import pallas as pl
from jax.experimental.pallas import tpu as pltpu
from jax.sharding import PartitionSpec as P

HEAD = 128
EPS = 1e-05
SCALE_LOG2 = (HEAD ** -0.5) * 1.4426950408889634
MESH = pl.DeviceIdType.MESH
BF16 = jnp.bfloat16
F32 = jnp.float32


def rcopy(src, dst, send, recv, t, v):
    return pltpu.make_async_remote_copy(
        src_ref=src, dst_ref=dst, send_sem=send, recv_sem=recv, device_id=(t, v), device_id_type=MESH
    )


def head_norm(heads, gain):
    mean_square = jnp.mean(heads * heads, axis=-1, keepdims=True)
    return heads * lax.rsqrt(mean_square + EPS) * gain


def column_tile(columns):
    lane = lax.broadcasted_iota(jnp.int32, (8, 128), 1)
    tile = jnp.zeros((8, 128), F32)
    for i, column in enumerate(columns):
        for k in range(32):
            tile = jnp.where(lane == 32 * i + k, column[8 * k : 8 * k + 8], tile)
    return tile


def kernel(
    text_hbm, vis_ref, gain_hbm, wq_hbm, wkv_hbm, qg_hbm, kg_hbm, wo_hbm, gate_hbm,
    out_ref,
    text_ref, gain_ref, qg_ref, kg_ref, gate_ref,
    text_s, text_all, wq, wk, vb, q_loc, q_heads, qbuf, kvst, kvb,
    o_send, t_send, o_recv, t_recv, o2, t2, d_all, t_all, att, att_all, wo_all, terms_send, terms_recv,
    loc, vsend, vrecv, wsend, wrecv, tsend, trecv, txsend, txrecv,
    qzsend, qzrecv, qsend, qrecv, kvsend, kvrecv, osend, orecv, ssend, srecv,
    dsend, drecv, t2send, t2recv, asend, arecv, axsend, axrecv,
    wzsend, wzrecv, wpsend, wprecv, wssend, wsrecv,
):
    t = lax.axis_index("text")
    v = lax.axis_index("vis")
    z = v // 2
    xl = v % 2
    c = t % 2
    half = t // 8
    g = t % 8
    vx = 2 * z + 1 - xl
    sib = t + 1 - 2 * c
    xh = (t // 2) % 2
    base = (t // 4) * 4
    xp = base + (1 - xh) * 2 + c
    up = (t + 4) % 16
    dn = (t + 12) % 16
    far = (t + 8) % 16
    col = t - c
    pcol = base + (1 - xh) * 2
    far_sib = (sib + 8) % 16
    cross = jnp.where((t // 4) % 2 == 0, dn, up)
    group = half * 8
    own_half = half == 0

    def at_z(zz):
        return 2 * zz + xl

    def each_z(body):
        def step(i, carry):
            body(lax.rem(z + 8 + jnp.where(i % 2 == 0, -(i // 2), (i + 1) // 2), 16), i)
            return carry

        lax.fori_loop(0, 15, step, 0)

    def nearest(i):
        bits = [(g // n % 2 + i // n % 2) % 2 for n in (1, 2, 4)]
        return bits[0] + 2 * bits[1] + 4 * bits[2]

    def lanes(i):
        return pl.ds(pl.multiple_of(i * 128, 128), 128)

    barrier = pltpu.get_barrier_semaphore()

    def greet(tt, vv):
        pl.semaphore_signal(barrier, inc=1, device_id=(tt, vv), device_id_type=MESH)

    def greet_group(i, carry):
        other = group + lax.rem(g + i, 8)
        greet(other, v)
        greet(other, vx)
        return carry

    each_z(lambda zz, i: greet(t, at_z(zz)))
    for other in (far, far_sib, cross):
        greet(other, v)
    lax.fori_loop(1, 8, greet_group, 0)
    greet(t, vx)

    small = [
        pltpu.make_async_copy(text_hbm, text_ref, loc.at[4]),
        pltpu.make_async_copy(gain_hbm.at[:, lanes(v)], gain_ref, loc.at[5]),
        pltpu.make_async_copy(qg_hbm, qg_ref, loc.at[6]),
        pltpu.make_async_copy(kg_hbm, kg_ref, loc.at[7]),
        pltpu.make_async_copy(gate_hbm, gate_ref, loc.at[8]),
    ]
    for copy in small:
        copy.start()
    own_tokens = pltpu.make_async_copy(vis_ref.at[pl.ds(c * 256, 256), :], vb.at[t], loc.at[0])
    own_wq = pltpu.make_async_copy(wq_hbm, wq, loc.at[1])
    own_wk = pltpu.make_async_copy(wkv_hbm, wk.at[:, lanes(c)], loc.at[2])
    own_tokens.start()
    own_wk.start()
    own_wq.start()

    for copy in small:
        copy.wait()
    text_s[...] = (text_ref[...].astype(F32) * gain_ref[...]).astype(BF16)
    text_all[xl, :, lanes(z)] = text_s[...]
    pl.semaphore_wait(barrier, 15 + 3 + 14 + 1)

    groups = ((10, 23),), ((7, 10),)

    def push_text(zz, i):
        stage = jnp.where(i < 3, 1, 0)
        rcopy(text_s, text_all.at[xl, :, lanes(z)], tsend, trecv.at[stage], t, at_z(zz)).start()

    each_z(push_text)

    def forward_text(stage):
        part = text_all.at[0, :, pl.ds(0, (12, 3)[stage] * 128)]
        rcopy(part, part, txsend, trecv.at[stage], t, vx).wait_recv()

        def forward(i, carry):
            mine = text_all.at[xl, :, lanes(lax.rem(z + i, 16))]
            rcopy(mine, mine, txsend, txrecv, t, vx).start()
            return carry

        for first, last in groups[stage]:
            lax.fori_loop(first, last, forward, 0)

    sends = []

    def piece(f, h):
        return vb.at[f, pl.ds(h * 128, 128), :]

    def send_block(f, h, target, src=None):
        copy = rcopy(
            piece(f, h) if src is None else src, piece(f, h),
            vsend.at[len(sends)], vrecv.at[f + 16 * h], target, v,
        )
        copy.start()
        sends.append(copy)

    def got(f, h):
        rcopy(piece(f, h), piece(f, h), vsend.at[0], vrecv.at[f + 16 * h], sib, v).wait_recv()

    def relay(f, h, *targets):
        got(f, h)
        for target in targets:
            send_block(f, h, target)

    for h in range(2):
        send_block(t, h, sib, vis_ref.at[pl.ds((1 - c) * 256 + h * 128, 128), :])
        for target in (up, dn, xp):
            send_block(t, h, target, vis_ref.at[pl.ds(c * 256 + h * 128, 128), :])
    w_out = rcopy(wkv_hbm, wk.at[:, lanes(c)], wsend, wrecv, sib, v)
    w_out.start()
    for h in range(2):
        relay(sib, h, up, dn, xp)

    up0, up1 = (col + 4) % 16, (col + 5) % 16
    dn0, dn1 = (col + 12) % 16, (col + 13) % 16
    far0, far1 = (col + 8) % 16, (col + 9) % 16
    pup0, pup1 = (pcol + 4) % 16, (pcol + 5) % 16
    pdn0, pdn1 = (pcol + 12) % 16, (pcol + 13) % 16
    pfar0, pfar1 = (pcol + 8) % 16, (pcol + 9) % 16

    def relays_first(h):
        relay(dn0, h, up)
        relay(up1, h, dn)
        relay(pcol, h, up)
        relay(pcol + 1, h, dn)

    def relays_second(h):
        relay(dn1, h, xp)
        relay(up0, h, xp)
        relay(pdn0, h, up)
        relay(pup1, h, dn)

    relays_first(0)
    forward_text(0)
    relays_first(1)
    forward_text(1)

    def project_text(q, parity):
        for k in range(8):
            weights = [
                wq[pl.ds(pl.multiple_of((4 * k + 2 * e + parity) * 128, 128), 128), :] for e in range(2)
            ]
            q = q + jnp.dot(
                text_all[parity, :, k * 256 : k * 256 + 256], jnp.concatenate(weights, axis=0),
                preferred_element_type=F32,
            )
        return q

    own_wq.wait()
    q = project_text(jnp.zeros((32, 128), F32), xl)
    text_other = text_all.at[1 - xl]
    rcopy(text_other, text_other, txsend, txrecv, t, vx).wait_recv()
    q = project_text(q, 1 - xl)
    q_loc[...] = head_norm(q, qg_ref[...]).astype(BF16)
    q_heads[z] = q_loc[...]
    each_z(
        lambda zz, i: rcopy(
            q_loc, q_heads.at[z], qzsend, qzrecv.at[z], t, at_z(zz)
        ).start()
    )

    w_rows = pl.ds(pl.multiple_of((t // 2) * 16, 16), 16)
    own_w = pltpu.make_async_copy(
        wo_hbm.at[w_rows, lanes(2 * z + c)], wo_all.at[c, z, w_rows, :], loc.at[3]
    )
    own_w.start()
    each_z(
        lambda zz, i: rcopy(
            wo_hbm.at[w_rows, lanes(2 * zz + c)], wo_all.at[c, z, w_rows, :],
            wzsend, wzrecv, t, at_z(zz),
        ).start()
    )

    for h in range(2):
        relays_second(h)

    def share_heads(i, carry):
        place = (g + i) % 2
        other = lax.rem(z // 2 + 8 + jnp.where(place == 0, -(i // 2), i // 2 + 1), 8)
        for e in range(2):
            zz = 2 * other + e

            @pl.when(zz != z)
            def _():
                rcopy(q_loc, q_heads.at[zz], qzsend, qzrecv.at[zz], t, vx).wait_recv()

        part = q_heads.at[pl.ds(2 * other, 2)]
        rcopy(part, qbuf.at[xl, g], qsend, qrecv.at[xl], group + other, vx).start()

        @pl.when(other != g)
        def _():
            rcopy(part, qbuf.at[xl, g], qsend, qrecv.at[xl], group + other, v).start()

        @pl.when(other == g)
        def _():
            qbuf[xl, g] = q_heads[pl.ds(2 * g, 2)]

        return carry

    lax.fori_loop(0, 4, share_heads, 0)

    own_tokens.wait()
    own_wk.wait()
    wk_other = wk.at[:, lanes(1 - c)]
    rcopy(wk_other, wk_other, wsend, wrecv, sib, v).wait_recv()
    kv_sends = []

    def project(h):
        for f in (pdn1, pup0, far0, far1, pfar0, pfar1):
            got(f, h)
        acc = jnp.zeros((128, 256), F32)
        for f in range(16):
            acc = acc + jnp.dot(
                vb[f, h * 128 : h * 128 + 128, :], wk[f * 256 : f * 256 + 256, :],
                preferred_element_type=F32,
            )
        raw = acc.astype(BF16).astype(F32)
        for n in range(2):
            part = raw[:, n * 128 : n * 128 + 128]
            normed = head_norm(part, kg_ref[...])
            kvst[h, n] = jnp.where(own_half, normed, part).astype(BF16)
        rows = pl.ds(pl.multiple_of(c * 256 + h * 128, 128), 128)
        for i, (n, target) in enumerate(((c, far), (1 - c, far_sib), (1 - c, sib))):
            copy = rcopy(
                kvst.at[h, n], kvb.at[half, rows, :], kvsend.at[3 * h + i], kvrecv.at[3 * h + i], target, v
            )
            copy.start()
            kv_sends.append(copy)
        kvb[half, rows, :] = kvst[h, c]

    project(0)
    lax.fori_loop(4, 8, share_heads, 0)
    project(1)

    def w_block(f):
        return wo_all.at[c, :, pl.ds(pl.multiple_of((f // 2) * 16, 16), 16), :]

    w_sends = []

    def w_send(f, *targets):
        for target in targets:
            copy = rcopy(w_block(f), w_block(f), wpsend.at[len(w_sends)], wprecv.at[f // 2], target, v)
            copy.start()
            w_sends.append(copy)

    def w_got(f):
        rcopy(w_block(f), w_block(f), wpsend.at[0], wprecv.at[f // 2], sib, v).wait_recv()

    w_landed = wo_all.at[c, pl.ds(0, 15), pl.ds(0, 16), :]
    own_w.wait()
    rcopy(w_landed, w_landed, wzsend, wzrecv, t, vx).wait_recv()

    q7 = qbuf.at[xl, pl.ds(0, 7)]
    rcopy(q7, q7, qsend, qrecv.at[xl], t, vx).wait_recv()
    q8 = qbuf.at[1 - xl]
    rcopy(q8, q8, qsend, qrecv.at[1 - xl], t, vx).wait_recv()
    for h in range(2):
        here = pl.ds(pl.multiple_of(c * 256 + h * 128, 128), 128)
        there = pl.ds(pl.multiple_of((1 - c) * 256 + h * 128, 128), 128)
        for i, rows in ((0, (1 - half, here)), (1, (1 - half, there)), (2, (half, there))):
            block = kvb.at[rows[0], rows[1], :]
            rcopy(block, block, kvsend.at[0], kvrecv.at[3 * h + i], sib, v).wait_recv()

    def attend(parity):
        columns = []
        for jj in range(2):
            scores = lax.dot_general(
                qbuf[parity, :, jj].reshape(256, 128), kvb[0], (((1,), (1,)), ((), ())),
                preferred_element_type=F32,
            )
            peak = jnp.max(scores, axis=-1, keepdims=True)
            probs = jnp.exp2((scores - peak) * SCALE_LOG2)
            columns += [peak * SCALE_LOG2, jnp.sum(probs, axis=-1, keepdims=True)]
            partial = jnp.dot(probs.astype(BF16), kvb[1], preferred_element_type=F32)
            o_send[parity, :, jj] = partial.astype(BF16).reshape(8, 32, 128)
        t_send[parity] = column_tile(columns)

    def send_partial(parity, rb, vv):
        rcopy(
            o_send.at[parity, rb], o_recv.at[xl, g], osend, orecv.at[xl, g], group + rb, vv
        ).start()
        rcopy(
            t_send.at[parity], t_recv.at[xl, g], ssend, srecv.at[xl, g], group + rb, vv
        ).start()

    def send_other(i, carry):
        send_partial(1 - xl, nearest(7 - i), vx)
        return carry

    def send_own(i, carry):
        send_partial(xl, nearest(8 - i), v)
        return carry

    attend(1 - xl)
    lax.fori_loop(0, 8, send_other, 0)
    attend(xl)
    lax.fori_loop(1, 8, send_own, 0)
    o_recv[xl, g] = o_send[xl, g]
    t_recv[xl, g] = t_send[xl]

    w_send(t, xp, far, up, dn)

    lane = lax.broadcasted_iota(jnp.int32, (8, 128), 1)
    sub = lax.broadcasted_iota(jnp.int32, (8, 128), 0)

    def merge(i, carry):
        src = lax.rem(z // 2 + 8 + jnp.where(i % 2 == 0, -(i // 2), (i + 1) // 2) + 4, 8)
        for x in range(2):

            @pl.when(jnp.logical_or(x != xl, src != g))
            def _():
                rcopy(o_recv.at[x, src], o_recv.at[x, src], osend, orecv.at[x, src], t, vx).wait_recv()
                rcopy(t_recv.at[x, src], t_recv.at[x, src], ssend, srecv.at[x, src], t, vx).wait_recv()

        shift = lax.rem(128 - 4 * g, 128)
        first = pltpu.roll(t_recv[0, src], shift, 1)
        second = pltpu.roll(t_recv[1, src], shift, 1)
        top = jnp.maximum(first, second)
        a = jnp.exp2(first - top)
        b = jnp.exp2(second - top)
        total = pltpu.roll(a, 32, 1) * first + pltpu.roll(b, 32, 1) * second
        for jj in range(2):
            zz = 2 * src + jj
            row = jnp.zeros((8, 128), F32)
            blocks = []
            for k in range(4):
                m, l = 64 * jj + k, 64 * jj + 32 + k
                row = jnp.where(lane == 8 * sub + k, top[:, m : m + 1], row)
                row = jnp.where(lane == 8 * sub + 4 + k, total[:, l : l + 1], row)
                rows = slice(8 * k, 8 * k + 8)
                blocks.append(
                    o_recv[0, src, jj].astype(F32)[rows] * a[:, m : m + 1]
                    + o_recv[1, src, jj].astype(F32)[rows] * b[:, m : m + 1]
                )
            o2[zz] = jnp.concatenate(blocks, axis=0).astype(BF16)
            t2[zz, 0:1, :] = jnp.sum(row, axis=0, keepdims=True)

            @pl.when(zz != z)
            def _():
                rcopy(o2.at[zz], d_all.at[z], dsend, drecv, t, at_z(zz)).start()
                rcopy(
                    t2.at[zz, pl.ds(0, 1), :], t_all.at[z, pl.ds(0, 1), :], t2send, t2recv, t, at_z(zz)
                ).start()

            @pl.when(zz == z)
            def _():
                d_all[z] = o2[zz]
                t_all[z, 0:1, :] = t2[zz, 0:1, :]

        return carry

    lax.fori_loop(0, 8, merge, 0)

    w_got(xp)
    w_send(xp, far, up, dn)

    for copy in (*sends, w_out, *kv_sends, *w_sends):
        copy.wait_send()
    z15 = att_all.at[:, pl.ds(0, 15 * 128)]
    rcopy(z15, z15, tsend, trecv.at[0], t, vx).wait_send()
    rcopy(text_all.at[0], text_all.at[0], txsend, txrecv, t, vx).wait_send()
    q15 = q_heads.at[pl.ds(0, 15)]
    rcopy(q15, q15, qzsend, qzrecv.at[0], t, vx).wait_send()
    for blocks in (q7, q8):
        rcopy(blocks, blocks, qsend, qrecv.at[xl], t, vx).wait_send()
    rcopy(w_landed, w_landed, wzsend, wzrecv, t, vx).wait_send()
    for blocks in (o_recv.at[0], o_recv.at[0, pl.ds(0, 7)]):
        rcopy(blocks, blocks, osend, orecv.at[0, 0], t, vx).wait_send()
    for blocks in (t_recv.at[0], t_recv.at[0, pl.ds(0, 7)]):
        rcopy(blocks, blocks, ssend, srecv.at[0, 0], t, vx).wait_send()

    d15, t15 = d_all.at[pl.ds(0, 15)], t_all.at[pl.ds(0, 15), pl.ds(0, 1), :]
    rcopy(t15, t15, t2send, t2recv, t, vx).wait_recv()
    rcopy(d15, d15, dsend, drecv, t, vx).wait_recv()
    top = t_all[0, 0:1, :]
    for s in range(1, 16):
        top = jnp.maximum(top, t_all[s, 0:1, :])

    def column(row, k):
        return jnp.sum(
            jnp.where(lane == 8 * sub + k, jnp.broadcast_to(row, (8, 128)), 0.0), axis=1, keepdims=True
        )

    den = jnp.zeros((1, 128), F32)
    num = [jnp.zeros((8, 128), F32) for _ in range(4)]
    for s in range(16):
        row = t_all[s, 0:1, :]
        w = jnp.exp2(row - top)
        den = den + w * pltpu.roll(row, 124, 1)
        block = d_all[s].astype(F32)
        for k in range(4):
            num[k] = num[k] + block[8 * k : 8 * k + 8] * column(w, k)
    attended = jnp.concatenate([num[k] / column(den, k) for k in range(4)], axis=0)
    att[...] = attended.astype(BF16)
    att_all[:, lanes(z)] = att[...]
    each_z(
        lambda zz, i: rcopy(att, att_all.at[:, lanes(z)], asend, arecv, t, at_z(zz)).start()
    )

    for f in (up, dn, far, pup0, pdn0, pfar0):
        w_got(f)
    w_sib = rcopy(wo_all.at[c], wo_all.at[c], wssend, wsrecv, sib, v)
    w_sib.start()

    rcopy(wo_all.at[1 - c], wo_all.at[1 - c], wssend, wsrecv, sib, v).wait_recv()

    rcopy(z15, z15, asend, arecv, t, vx).wait_recv()

    def project_out(parity):
        terms = jnp.zeros((32, 128), F32)
        for k in range(8):
            terms = terms + jnp.dot(
                att_all[:, k * 256 : k * 256 + 256],
                wo_all[parity, 2 * k : 2 * k + 2].reshape(256, 128),
                preferred_element_type=F32,
            )
        return terms

    terms_send[...] = project_out(1 - xl)
    terms_x = rcopy(terms_send, terms_recv, axsend, axrecv, t, vx)
    terms_x.start()
    mine = project_out(xl)
    terms_x.wait_recv()
    out_ref[...] = (jnp.tanh(gate_ref[...]) * (mine + terms_recv[...])).astype(BF16)
    w_sib.wait_send()
    rcopy(z15, z15, asend, arecv, t, vx).wait_send()
    terms_x.wait_send()
    rcopy(d15, d15, dsend, drecv, t, vx).wait_send()
    rcopy(t15, t15, t2send, t2recv, t, vx).wait_send()


def on_device(
    text_rows, visual, norm_gain, q_weight, key_value_weight, q_gain, k_gain, out_weight, attn_gate
):
    vmem = pl.BlockSpec(memory_space=pltpu.VMEM)
    hbm = pl.BlockSpec(memory_space=pl.ANY)
    dma = pltpu.SemaphoreType.DMA
    one = dma(())
    buffers = [
        pltpu.VMEM(*buffer)
        for buffer in (
            ((32, 128), BF16),
            ((1, 128), F32),
            ((1, 128), F32),
            ((1, 128), F32),
            ((1, 1), F32),
            ((32, 128), BF16),
            ((2, 32, 2048), BF16),
            ((4096, 128), BF16),
            ((4096, 256), BF16),
            ((16, 256, 256), BF16),
            ((32, 128), BF16),
            ((16, 32, 128), BF16),
            ((2, 8, 2, 32, 128), BF16),
            ((2, 2, 128, 128), BF16),
            ((2, 512, 128), BF16),
            ((2, 8, 2, 32, 128), BF16),
            ((2, 8, 128), F32),
            ((2, 8, 2, 32, 128), BF16),
            ((2, 8, 8, 128), F32),
            ((16, 32, 128), BF16),
            ((16, 8, 128), F32),
            ((16, 32, 128), BF16),
            ((16, 8, 128), F32),
            ((32, 128), BF16),
            ((32, 2048), BF16),
            ((2, 16, 128, 128), BF16),
            ((32, 128), F32),
            ((32, 128), F32),
        )
    ]
    semaphores = [
        dma((9,)),
        dma((30,)), dma((32,)),
        one, one,
        one, dma((2,)), one, one,
        one, dma((16,)), one, dma((2,)),
        dma((6,)), dma((6,)),
        one, dma((2, 8)), one, dma((2, 8)),
        one, one, one, one,
        one, one, one, one,
        one, one, dma((7,)), dma((8,)), one, one,
    ]
    return pl.pallas_call(
        kernel,
        out_shape=jax.ShapeDtypeStruct((32, 128), BF16),
        in_specs=[hbm] * 9,
        out_specs=vmem,
        scratch_shapes=buffers + semaphores,
        compiler_params=pltpu.CompilerParams(
            collective_id=0, has_side_effects=True, vmem_limit_bytes=60 * 1024 * 1024
        ),
    )(
        text_rows, visual, norm_gain.reshape(1, -1), q_weight, key_value_weight,
        q_gain.reshape(1, -1), k_gain.reshape(1, -1), out_weight, attn_gate.reshape(1, 1),
    )


def solution(mesh):
    placed = (
        P("text", "vis"),
        P("vis", "text"),
        P(),
        P(None, "vis"),
        P(None, "text"),
        P(),
        P(),
        P("vis", None),
        P(),
    )
    return jax.shard_map(
        on_device, mesh=mesh, in_specs=placed, out_specs=P("text", "vis"), check_vma=False
    )
```

```python
import jax
import jax.numpy as jnp
from jax import lax
from jax.experimental import pallas as pl
from jax.experimental.pallas import tpu as pltpu
from jax.sharding import PartitionSpec as P

HEAD = 128
EPS = 1e-05
SCALE_LOG2 = (HEAD ** -0.5) * 1.4426950408889634
MESH = pl.DeviceIdType.MESH
BF16 = jnp.bfloat16
F32 = jnp.float32


def rcopy(src, dst, send, recv, t, v):
    return pltpu.make_async_remote_copy(
        src_ref=src, dst_ref=dst, send_sem=send, recv_sem=recv, device_id=(t, v), device_id_type=MESH
    )


def head_norm(heads, gain):
    mean_square = jnp.mean(heads * heads, axis=-1, keepdims=True)
    return heads * lax.rsqrt(mean_square + EPS) * gain


def column_tile(columns):
    lane = lax.broadcasted_iota(jnp.int32, (8, 128), 1)
    tile = jnp.zeros((8, 128), F32)
    for i, column in enumerate(columns):
        for k in range(32):
            tile = jnp.where(lane == 32 * i + k, column[8 * k : 8 * k + 8], tile)
    return tile


def kernel(
    text_hbm, vis_ref, gain_hbm, wq_hbm, wkv_hbm, qg_hbm, kg_hbm, wo_hbm, gate_hbm,
    out_ref,
    text_ref, gain_ref, qg_ref, kg_ref, gate_ref,
    text_s, text_all, wq, wk, vb, q_loc, q_heads, qbuf, kvst, kvb,
    o_send, t_send, o_recv, t_recv, o2, t2, d_all, t_all, att, att_all, wo_all, terms_send, terms_recv,
    loc, vsend, vrecv, wsend, wrecv, tsend, trecv, txsend, txrecv,
    qzsend, qzrecv, qsend, qrecv, kvsend, kvrecv, osend, orecv, ssend, srecv,
    dsend, drecv, t2send, t2recv, asend, arecv, axsend, axrecv,
    wzsend, wzrecv, wpsend, wprecv, wssend, wsrecv,
):
    t = lax.axis_index("text")
    v = lax.axis_index("vis")
    z = v // 2
    xl = v % 2
    c = t % 2
    half = t // 8
    g = t % 8
    vx = 2 * z + 1 - xl
    sib = t + 1 - 2 * c
    xh = (t // 2) % 2
    base = (t // 4) * 4
    xp = base + (1 - xh) * 2 + c
    up = (t + 4) % 16
    dn = (t + 12) % 16
    far = (t + 8) % 16
    col = t - c
    pcol = base + (1 - xh) * 2
    far_sib = (sib + 8) % 16
    cross = jnp.where((t // 4) % 2 == 0, dn, up)
    group = half * 8
    own_half = half == 0

    def at_z(zz):
        return 2 * zz + xl

    def each_z(body):
        def step(i, carry):
            body(lax.rem(z + 8 + jnp.where(i % 2 == 0, -(i // 2), (i + 1) // 2), 16), i)
            return carry

        lax.fori_loop(0, 15, step, 0)

    def nearest(i):
        bits = [(g // n % 2 + i // n % 2) % 2 for n in (1, 2, 4)]
        return bits[0] + 2 * bits[1] + 4 * bits[2]

    def lanes(i):
        return pl.ds(pl.multiple_of(i * 128, 128), 128)

    barrier = pltpu.get_barrier_semaphore()

    def greet(tt, vv):
        pl.semaphore_signal(barrier, inc=1, device_id=(tt, vv), device_id_type=MESH)

    def greet_group(i, carry):
        other = group + lax.rem(g + i, 8)
        greet(other, v)
        greet(other, vx)
        return carry

    each_z(lambda zz, i: greet(t, at_z(zz)))
    for other in (far, far_sib, cross):
        greet(other, v)
    lax.fori_loop(1, 8, greet_group, 0)
    greet(t, vx)

    small = [
        pltpu.make_async_copy(text_hbm, text_ref, loc.at[4]),
        pltpu.make_async_copy(gain_hbm.at[:, lanes(v)], gain_ref, loc.at[5]),
        pltpu.make_async_copy(qg_hbm, qg_ref, loc.at[6]),
        pltpu.make_async_copy(kg_hbm, kg_ref, loc.at[7]),
        pltpu.make_async_copy(gate_hbm, gate_ref, loc.at[8]),
    ]
    for copy in small:
        copy.start()
    own_tokens = pltpu.make_async_copy(vis_ref.at[pl.ds(c * 256, 256), :], vb.at[t], loc.at[0])
    own_wq = pltpu.make_async_copy(wq_hbm, wq, loc.at[1])
    own_wk = pltpu.make_async_copy(wkv_hbm, wk.at[:, lanes(c)], loc.at[2])
    own_tokens.start()
    own_wk.start()
    own_wq.start()

    for copy in small:
        copy.wait()
    text_s[...] = (text_ref[...].astype(F32) * gain_ref[...]).astype(BF16)
    text_all[xl, :, lanes(z)] = text_s[...]
    pl.semaphore_wait(barrier, 15 + 3 + 14 + 1)

    groups = ((10, 23),), ((7, 10),)

    def push_text(zz, i):
        stage = jnp.where(i < 3, 1, 0)
        rcopy(text_s, text_all.at[xl, :, lanes(z)], tsend, trecv.at[stage], t, at_z(zz)).start()

    each_z(push_text)

    def forward_text(stage):
        part = text_all.at[0, :, pl.ds(0, (12, 3)[stage] * 128)]
        rcopy(part, part, txsend, trecv.at[stage], t, vx).wait_recv()

        def forward(i, carry):
            mine = text_all.at[xl, :, lanes(lax.rem(z + i, 16))]
            rcopy(mine, mine, txsend, txrecv, t, vx).start()
            return carry

        for first, last in groups[stage]:
            lax.fori_loop(first, last, forward, 0)

    sends = []

    def piece(f, h):
        return vb.at[f, pl.ds(h * 128, 128), :]

    def send_block(f, h, target, src=None):
        copy = rcopy(
            piece(f, h) if src is None else src, piece(f, h),
            vsend.at[len(sends)], vrecv.at[f + 16 * h], target, v,
        )
        copy.start()
        sends.append(copy)

    def got(f, h):
        rcopy(piece(f, h), piece(f, h), vsend.at[0], vrecv.at[f + 16 * h], sib, v).wait_recv()

    def relay(f, h, *targets):
        got(f, h)
        for target in targets:
            send_block(f, h, target)

    for h in range(2):
        send_block(t, h, sib, vis_ref.at[pl.ds((1 - c) * 256 + h * 128, 128), :])
        for target in (xp, up, dn):
            send_block(t, h, target, vis_ref.at[pl.ds(c * 256 + h * 128, 128), :])
    w_out = rcopy(wkv_hbm, wk.at[:, lanes(c)], wsend, wrecv, sib, v)
    w_out.start()
    for h in range(2):
        relay(sib, h, xp, up, dn)

    up0, up1 = (col + 4) % 16, (col + 5) % 16
    dn0, dn1 = (col + 12) % 16, (col + 13) % 16
    far0, far1 = (col + 8) % 16, (col + 9) % 16
    pup0, pup1 = (pcol + 4) % 16, (pcol + 5) % 16
    pdn0, pdn1 = (pcol + 12) % 16, (pcol + 13) % 16
    pfar0, pfar1 = (pcol + 8) % 16, (pcol + 9) % 16

    def relays_first(h):
        relay(dn0, h, up)
        relay(up1, h, dn)
        relay(pcol, h, up)
        relay(pcol + 1, h, dn)

    def relays_second(h):
        relay(dn1, h, xp)
        relay(up0, h, xp)
        relay(pdn0, h, up)
        relay(pup1, h, dn)

    relays_first(0)
    forward_text(0)
    relays_first(1)
    forward_text(1)

    def project_text(q, parity):
        for k in range(8):
            weights = [
                wq[pl.ds(pl.multiple_of((4 * k + 2 * e + parity) * 128, 128), 128), :] for e in range(2)
            ]
            q = q + jnp.dot(
                text_all[parity, :, k * 256 : k * 256 + 256], jnp.concatenate(weights, axis=0),
                preferred_element_type=F32,
            )
        return q

    own_wq.wait()
    q = project_text(jnp.zeros((32, 128), F32), xl)
    text_other = text_all.at[1 - xl]
    rcopy(text_other, text_other, txsend, txrecv, t, vx).wait_recv()
    q = project_text(q, 1 - xl)
    q_loc[...] = head_norm(q, qg_ref[...]).astype(BF16)
    q_heads[z] = q_loc[...]
    each_z(
        lambda zz, i: rcopy(
            q_loc, q_heads.at[z], qzsend, qzrecv.at[z], t, at_z(zz)
        ).start()
    )

    w_rows = pl.ds(pl.multiple_of((t // 2) * 16, 16), 16)
    own_w = pltpu.make_async_copy(
        wo_hbm.at[w_rows, lanes(2 * z + c)], wo_all.at[c, z, w_rows, :], loc.at[3]
    )
    own_w.start()
    each_z(
        lambda zz, i: rcopy(
            wo_hbm.at[w_rows, lanes(2 * zz + c)], wo_all.at[c, z, w_rows, :],
            wzsend, wzrecv, t, at_z(zz),
        ).start()
    )

    for h in range(2):
        relays_second(h)

    def share_heads(i, carry):
        place = (g + i) % 2
        other = lax.rem(z // 2 + 8 + jnp.where(place == 0, -(i // 2), i // 2 + 1), 8)
        for e in range(2):
            zz = 2 * other + e

            @pl.when(zz != z)
            def _():
                rcopy(q_loc, q_heads.at[zz], qzsend, qzrecv.at[zz], t, vx).wait_recv()

        part = q_heads.at[pl.ds(2 * other, 2)]
        rcopy(part, qbuf.at[xl, g], qsend, qrecv.at[xl], group + other, vx).start()

        @pl.when(other != g)
        def _():
            rcopy(part, qbuf.at[xl, g], qsend, qrecv.at[xl], group + other, v).start()

        @pl.when(other == g)
        def _():
            qbuf[xl, g] = q_heads[pl.ds(2 * g, 2)]

        return carry

    lax.fori_loop(0, 4, share_heads, 0)

    own_tokens.wait()
    own_wk.wait()
    wk_other = wk.at[:, lanes(1 - c)]
    rcopy(wk_other, wk_other, wsend, wrecv, sib, v).wait_recv()
    kv_sends = []

    def project(h):
        for f in (pdn1, pup0, far0, far1, pfar0, pfar1):
            got(f, h)
        acc = jnp.zeros((128, 256), F32)
        for f in range(16):
            acc = acc + jnp.dot(
                vb[f, h * 128 : h * 128 + 128, :], wk[f * 256 : f * 256 + 256, :],
                preferred_element_type=F32,
            )
        raw = acc.astype(BF16).astype(F32)
        for n in range(2):
            part = raw[:, n * 128 : n * 128 + 128]
            normed = head_norm(part, kg_ref[...])
            kvst[h, n] = jnp.where(own_half, normed, part).astype(BF16)
        rows = pl.ds(pl.multiple_of(c * 256 + h * 128, 128), 128)
        for i, (n, target) in enumerate(((c, far), (1 - c, far_sib), (1 - c, sib))):
            copy = rcopy(
                kvst.at[h, n], kvb.at[half, rows, :], kvsend.at[3 * h + i], kvrecv.at[3 * h + i], target, v
            )
            copy.start()
            kv_sends.append(copy)
        kvb[half, rows, :] = kvst[h, c]

    project(0)
    lax.fori_loop(4, 8, share_heads, 0)
    project(1)

    def w_block(f):
        return wo_all.at[c, :, pl.ds(pl.multiple_of((f // 2) * 16, 16), 16), :]

    w_sends = []

    def w_send(f, *targets):
        for target in targets:
            copy = rcopy(w_block(f), w_block(f), wpsend.at[len(w_sends)], wprecv.at[f // 2], target, v)
            copy.start()
            w_sends.append(copy)

    def w_got(f):
        rcopy(w_block(f), w_block(f), wpsend.at[0], wprecv.at[f // 2], sib, v).wait_recv()

    w_landed = wo_all.at[c, pl.ds(0, 15), pl.ds(0, 16), :]
    own_w.wait()
    rcopy(w_landed, w_landed, wzsend, wzrecv, t, vx).wait_recv()

    q7 = qbuf.at[xl, pl.ds(0, 7)]
    rcopy(q7, q7, qsend, qrecv.at[xl], t, vx).wait_recv()
    q8 = qbuf.at[1 - xl]
    rcopy(q8, q8, qsend, qrecv.at[1 - xl], t, vx).wait_recv()
    for h in range(2):
        here = pl.ds(pl.multiple_of(c * 256 + h * 128, 128), 128)
        there = pl.ds(pl.multiple_of((1 - c) * 256 + h * 128, 128), 128)
        for i, rows in ((0, (1 - half, here)), (1, (1 - half, there)), (2, (half, there))):
            block = kvb.at[rows[0], rows[1], :]
            rcopy(block, block, kvsend.at[0], kvrecv.at[3 * h + i], sib, v).wait_recv()

    def attend(parity):
        columns = []
        for jj in range(2):
            scores = lax.dot_general(
                qbuf[parity, :, jj].reshape(256, 128), kvb[0], (((1,), (1,)), ((), ())),
                preferred_element_type=F32,
            )
            peak = jnp.max(scores, axis=-1, keepdims=True)
            probs = jnp.exp2((scores - peak) * SCALE_LOG2)
            columns += [peak * SCALE_LOG2, jnp.sum(probs, axis=-1, keepdims=True)]
            partial = jnp.dot(probs.astype(BF16), kvb[1], preferred_element_type=F32)
            o_send[parity, :, jj] = partial.astype(BF16).reshape(8, 32, 128)
        t_send[parity] = column_tile(columns)

    def send_partial(parity, rb, vv):
        rcopy(
            o_send.at[parity, rb], o_recv.at[xl, g], osend, orecv.at[xl, g], group + rb, vv
        ).start()
        rcopy(
            t_send.at[parity], t_recv.at[xl, g], ssend, srecv.at[xl, g], group + rb, vv
        ).start()

    def send_other(i, carry):
        send_partial(1 - xl, nearest(7 - i), vx)
        return carry

    def send_own(i, carry):
        send_partial(xl, nearest(8 - i), v)
        return carry

    attend(1 - xl)
    lax.fori_loop(0, 8, send_other, 0)
    attend(xl)
    lax.fori_loop(1, 8, send_own, 0)
    o_recv[xl, g] = o_send[xl, g]
    t_recv[xl, g] = t_send[xl]

    w_send(t, xp, far, up, dn)

    lane = lax.broadcasted_iota(jnp.int32, (8, 128), 1)
    sub = lax.broadcasted_iota(jnp.int32, (8, 128), 0)

    def merge(i, carry):
        src = lax.rem(z // 2 + 8 + jnp.where(i % 2 == 0, -(i // 2), (i + 1) // 2) + 4, 8)
        for x in range(2):

            @pl.when(jnp.logical_or(x != xl, src != g))
            def _():
                rcopy(o_recv.at[x, src], o_recv.at[x, src], osend, orecv.at[x, src], t, vx).wait_recv()
                rcopy(t_recv.at[x, src], t_recv.at[x, src], ssend, srecv.at[x, src], t, vx).wait_recv()

        shift = lax.rem(128 - 4 * g, 128)
        first = pltpu.roll(t_recv[0, src], shift, 1)
        second = pltpu.roll(t_recv[1, src], shift, 1)
        top = jnp.maximum(first, second)
        a = jnp.exp2(first - top)
        b = jnp.exp2(second - top)
        total = pltpu.roll(a, 32, 1) * first + pltpu.roll(b, 32, 1) * second
        for jj in range(2):
            zz = 2 * src + jj
            row = jnp.zeros((8, 128), F32)
            blocks = []
            for k in range(4):
                m, l = 64 * jj + k, 64 * jj + 32 + k
                row = jnp.where(lane == 8 * sub + k, top[:, m : m + 1], row)
                row = jnp.where(lane == 8 * sub + 4 + k, total[:, l : l + 1], row)
                rows = slice(8 * k, 8 * k + 8)
                blocks.append(
                    o_recv[0, src, jj].astype(F32)[rows] * a[:, m : m + 1]
                    + o_recv[1, src, jj].astype(F32)[rows] * b[:, m : m + 1]
                )
            o2[zz] = jnp.concatenate(blocks, axis=0).astype(BF16)
            t2[zz, 0:1, :] = jnp.sum(row, axis=0, keepdims=True)

            @pl.when(zz != z)
            def _():
                rcopy(o2.at[zz], d_all.at[z], dsend, drecv, t, at_z(zz)).start()
                rcopy(
                    t2.at[zz, pl.ds(0, 1), :], t_all.at[z, pl.ds(0, 1), :], t2send, t2recv, t, at_z(zz)
                ).start()

            @pl.when(zz == z)
            def _():
                d_all[z] = o2[zz]
                t_all[z, 0:1, :] = t2[zz, 0:1, :]

        return carry

    lax.fori_loop(0, 8, merge, 0)

    w_got(xp)
    w_send(xp, far, up, dn)

    for copy in (*sends, w_out, *kv_sends, *w_sends):
        copy.wait_send()
    z15 = att_all.at[:, pl.ds(0, 15 * 128)]
    rcopy(z15, z15, tsend, trecv.at[0], t, vx).wait_send()
    rcopy(text_all.at[0], text_all.at[0], txsend, txrecv, t, vx).wait_send()
    q15 = q_heads.at[pl.ds(0, 15)]
    rcopy(q15, q15, qzsend, qzrecv.at[0], t, vx).wait_send()
    for blocks in (q7, q8):
        rcopy(blocks, blocks, qsend, qrecv.at[xl], t, vx).wait_send()
    rcopy(w_landed, w_landed, wzsend, wzrecv, t, vx).wait_send()
    for blocks in (o_recv.at[0], o_recv.at[0, pl.ds(0, 7)]):
        rcopy(blocks, blocks, osend, orecv.at[0, 0], t, vx).wait_send()
    for blocks in (t_recv.at[0], t_recv.at[0, pl.ds(0, 7)]):
        rcopy(blocks, blocks, ssend, srecv.at[0, 0], t, vx).wait_send()

    d15, t15 = d_all.at[pl.ds(0, 15)], t_all.at[pl.ds(0, 15), pl.ds(0, 1), :]
    rcopy(t15, t15, t2send, t2recv, t, vx).wait_recv()
    rcopy(d15, d15, dsend, drecv, t, vx).wait_recv()
    top = t_all[0, 0:1, :]
    for s in range(1, 16):
        top = jnp.maximum(top, t_all[s, 0:1, :])

    def column(row, k):
        return jnp.sum(
            jnp.where(lane == 8 * sub + k, jnp.broadcast_to(row, (8, 128)), 0.0), axis=1, keepdims=True
        )

    den = jnp.zeros((1, 128), F32)
    num = [jnp.zeros((8, 128), F32) for _ in range(4)]
    for s in range(16):
        row = t_all[s, 0:1, :]
        w = jnp.exp2(row - top)
        den = den + w * pltpu.roll(row, 124, 1)
        block = d_all[s].astype(F32)
        for k in range(4):
            num[k] = num[k] + block[8 * k : 8 * k + 8] * column(w, k)
    attended = jnp.concatenate([num[k] / column(den, k) for k in range(4)], axis=0)
    att[...] = attended.astype(BF16)
    att_all[:, lanes(z)] = att[...]
    each_z(
        lambda zz, i: rcopy(att, att_all.at[:, lanes(z)], asend, arecv, t, at_z(zz)).start()
    )

    for f in (up, dn, far, pup0, pdn0, pfar0):
        w_got(f)
    w_sib = rcopy(wo_all.at[c], wo_all.at[c], wssend, wsrecv, sib, v)
    w_sib.start()

    rcopy(wo_all.at[1 - c], wo_all.at[1 - c], wssend, wsrecv, sib, v).wait_recv()

    rcopy(z15, z15, asend, arecv, t, vx).wait_recv()

    def project_out(parity):
        terms = jnp.zeros((32, 128), F32)
        for k in range(8):
            terms = terms + jnp.dot(
                att_all[:, k * 256 : k * 256 + 256],
                wo_all[parity, 2 * k : 2 * k + 2].reshape(256, 128),
                preferred_element_type=F32,
            )
        return terms

    terms_send[...] = project_out(1 - xl)
    terms_x = rcopy(terms_send, terms_recv, axsend, axrecv, t, vx)
    terms_x.start()
    mine = project_out(xl)
    terms_x.wait_recv()
    out_ref[...] = (jnp.tanh(gate_ref[...]) * (mine + terms_recv[...])).astype(BF16)
    w_sib.wait_send()
    rcopy(z15, z15, asend, arecv, t, vx).wait_send()
    terms_x.wait_send()
    rcopy(d15, d15, dsend, drecv, t, vx).wait_send()
    rcopy(t15, t15, t2send, t2recv, t, vx).wait_send()


def on_device(
    text_rows, visual, norm_gain, q_weight, key_value_weight, q_gain, k_gain, out_weight, attn_gate
):
    vmem = pl.BlockSpec(memory_space=pltpu.VMEM)
    hbm = pl.BlockSpec(memory_space=pl.ANY)
    dma = pltpu.SemaphoreType.DMA
    one = dma(())
    buffers = [
        pltpu.VMEM(*buffer)
        for buffer in (
            ((32, 128), BF16),
            ((1, 128), F32),
            ((1, 128), F32),
            ((1, 128), F32),
            ((1, 1), F32),
            ((32, 128), BF16),
            ((2, 32, 2048), BF16),
            ((4096, 128), BF16),
            ((4096, 256), BF16),
            ((16, 256, 256), BF16),
            ((32, 128), BF16),
            ((16, 32, 128), BF16),
            ((2, 8, 2, 32, 128), BF16),
            ((2, 2, 128, 128), BF16),
            ((2, 512, 128), BF16),
            ((2, 8, 2, 32, 128), BF16),
            ((2, 8, 128), F32),
            ((2, 8, 2, 32, 128), BF16),
            ((2, 8, 8, 128), F32),
            ((16, 32, 128), BF16),
            ((16, 8, 128), F32),
            ((16, 32, 128), BF16),
            ((16, 8, 128), F32),
            ((32, 128), BF16),
            ((32, 2048), BF16),
            ((2, 16, 128, 128), BF16),
            ((32, 128), F32),
            ((32, 128), F32),
        )
    ]
    semaphores = [
        dma((9,)),
        dma((30,)), dma((32,)),
        one, one,
        one, dma((2,)), one, one,
        one, dma((16,)), one, dma((2,)),
        dma((6,)), dma((6,)),
        one, dma((2, 8)), one, dma((2, 8)),
        one, one, one, one,
        one, one, one, one,
        one, one, dma((7,)), dma((8,)), one, one,
    ]
    return pl.pallas_call(
        kernel,
        out_shape=jax.ShapeDtypeStruct((32, 128), BF16),
        in_specs=[hbm] * 9,
        out_specs=vmem,
        scratch_shapes=buffers + semaphores,
        compiler_params=pltpu.CompilerParams(
            collective_id=0, has_side_effects=True, vmem_limit_bytes=60 * 1024 * 1024
        ),
    )(
        text_rows, visual, norm_gain.reshape(1, -1), q_weight, key_value_weight,
        q_gain.reshape(1, -1), k_gain.reshape(1, -1), out_weight, attn_gate.reshape(1, 1),
    )


def solution(mesh):
    placed = (
        P("text", "vis"),
        P("vis", "text"),
        P(),
        P(None, "vis"),
        P(None, "text"),
        P(),
        P(),
        P("vis", None),
        P(),
    )
    return jax.shard_map(
        on_device, mesh=mesh, in_specs=placed, out_specs=P("text", "vis"), check_vma=False
    )
```
